256 devices in a mesh: node: 32 (over x, z), local: 8 (over y, core).
Axes of the slice: x: 4, y: 4, z: 8, core: 2. Of those that a mesh axis runs over, the one named last changes fastest.
Arguments:
- tokens: bfloat16 [32768, 3584], P(('node', 'local')), may hold values from -6 to 6
- expert_ids: int32 [32768, 4], P(('node', 'local')), may hold values from 0 to 127, as said below
- gate_weights: bfloat16 [32768, 4], P(('node', 'local')), may hold values from 0.099609375 to 1
- w_gate: bfloat16 [256, 3584, 512], P(('node', 'local')), may hold values from -0.09375 to 0.09375
- w_up: bfloat16 [256, 3584, 512], P(('node', 'local')), may hold values from -0.09375 to 0.09375
- w_down: bfloat16 [256, 512, 3584], P(('node', 'local')), may hold values from -0.1875 to 0.1875
Outputs:
- mixed: bfloat16 [32768, 3584], P(('node', 'local'))
The draws below stay inside these ranges and needn't reach their ends.
Inputs may be any that keep to these rules, and one draw needn't show every extreme that they name: `expert_ids`: each row names 4 different experts, two on each of two different nodes (the node of expert e is e // 4); among the rows of one device no expert is named by more than 5 rows.
All inputs are finite; a program needn't handle non-finite values.
Results may differ from the reference program's by a relative error of at most 0.0065.
Values may be sent and summed in bfloat16 or wider, within the bound.
No kernel may reach another device: no remote copies, remote signals or barrier semaphores. Data moves between devices by JAX's collectives and lax.ppermute only.
A program may use at most 192 MiB of HBM per device.

```python
import jax
import jax.numpy as jnp
from jax import lax

D = 3584
FF = 1024
TOP = 4
TOK_DEV = 128
FF_HALF = 512
EXP_NODE = 4
CAP = 5
TOKENS = 32768
SHARDS = 256
N_NODE = 32


def draw_expert_ids(key, part):
    shared_key = jax.random.fold_in(key, 17)
    device_base = jax.random.fold_in(key, 29)
    node_order = jax.random.permutation(shared_key, N_NODE).astype(jnp.int32)
    device_count = TOKENS // TOK_DEV
    base_load = 2 * TOK_DEV // N_NODE
    delta_load = TOK_DEV // (2 * N_NODE)
    groups = N_NODE // 4

    def one_device(device):
        dev_key = jax.random.fold_in(device_base, device)
        keys = jax.random.split(dev_key, 4)
        group_keys = jax.random.split(keys[0], groups)
        rest = jax.vmap(lambda inner: jax.random.permutation(inner, 3))(group_keys).astype(jnp.int32)
        options = jnp.array([0, 0, -1], jnp.int32)
        rest_loads = base_load + delta_load * options[rest]
        hot_loads = jnp.full((groups, 1), base_load + delta_load, jnp.int32)
        loads = jnp.concatenate([hot_loads, rest_loads], axis=1).reshape(N_NODE)
        ends = jnp.cumsum(loads)
        starts = ends - loads
        visit = jnp.arange(2 * TOK_DEV, dtype=jnp.int32)
        block = jnp.sum((visit[:, None] >= ends[None, :]).astype(jnp.int32), axis=1)
        offset = visit - starts[block]
        node = node_order[block]
        labels = jax.vmap(lambda inner: jax.random.permutation(inner, EXP_NODE))(jax.random.split(keys[1], N_NODE)).astype(jnp.int32)
        first = labels[node, offset % EXP_NODE]
        second = labels[node, (offset + EXP_NODE // 2) % EXP_NODE]
        paired = jnp.stack([node * EXP_NODE + first, node * EXP_NODE + second], axis=1)
        rows = jnp.concatenate([paired[:TOK_DEV], paired[TOK_DEV:]], axis=1)
        scores = jax.random.randint(keys[2], (TOK_DEV, TOP), 0, 1024) * TOP + jnp.arange(TOP, dtype=jnp.int32)[None, :]
        column_order = jnp.argsort(scores, axis=1, stable=True)
        rows = jnp.take_along_axis(rows, column_order, axis=1)
        token_order = jax.random.permutation(keys[3], TOK_DEV)
        return rows[token_order]
    every = jax.vmap(one_device)(jnp.arange(device_count, dtype=jnp.int32))
    return every.reshape(device_count * TOK_DEV, TOP).astype(jnp.int32)


def levels(stream_key, extent, shards, least, largest):
    loudness, own = 1.0, jax.random.fold_in(stream_key, 6)
    for position, blocks in shards:
        heights = jnp.exp(jax.random.uniform(jax.random.fold_in(own, position), (blocks,), jnp.float32, least / len(shards), largest / len(shards)))
        loudness = loudness * jnp.repeat(heights, extent[position] // blocks).reshape([-1 if axis == position else 1 for axis in range(len(extent))])
    return loudness


def noise(key, dims, scale, reach, shards=(), kind=jnp.bfloat16):
    values = jax.random.normal(key, dims, jnp.float32) * scale
    if len(shards) > 0:
        values = levels(key, dims, shards, -0.22, 0.18) * values
    return jnp.clip(values, min=-reach, max=reach).astype(kind)


def setup_inputs(seed: int = 0) -> dict:
    splits = jax.random.split(jax.random.key(seed), 7)
    return {
        "tokens": noise(splits[0], (TOKENS, D), 1.0, 6.0, ((0, 256),)),
        "expert_ids": draw_expert_ids(jax.random.fold_in(splits[6], 71), 0),
        "gate_weights": jnp.clip(0.099609375 + 0.9003906 * jax.random.uniform(splits[2], (TOKENS, TOP), jnp.float32) ** levels(splits[2], (TOKENS, TOP), ((0, 256),), -0.2, 0.2), 0.099609375, 1.0).astype(jnp.bfloat16),
        "w_gate": noise(splits[3], (SHARDS, D, FF_HALF), D ** -0.5, 0.09375, ((0, 256),)),
        "w_up": noise(splits[4], (SHARDS, D, FF_HALF), D ** -0.5, 0.09375, ((0, 256),)),
        "w_down": noise(splits[5], (SHARDS, FF_HALF, D), FF ** -0.5, 0.1875, ((0, 256),)),
    }


def expert_rows(expert, tokens, expert_ids, gate_weights, w_gate, w_up, w_down):
    hit_mask = expert_ids == expert
    limit = (TOKENS // TOK_DEV) * CAP
    any_hit = jnp.any(hit_mask, axis=1)
    row_index = jnp.nonzero(any_hit, size=limit, fill_value=0)[0]
    live_rows = jnp.arange(limit) < jnp.sum(any_hit.astype(jnp.int32))
    gate_row = jnp.sum(jnp.where(hit_mask, gate_weights.astype(jnp.float32), jnp.float32(0.0)), axis=1)[row_index]
    gate_row = jnp.where(live_rows, gate_row, jnp.float32(0.0))
    picked = tokens[row_index]
    gate_full = jnp.concatenate([w_gate[2 * expert], w_gate[2 * expert + 1]], axis=1)
    up_full = jnp.concatenate([w_up[2 * expert], w_up[2 * expert + 1]], axis=1)
    gate_part = jnp.dot(picked, gate_full, preferred_element_type=jnp.float32)
    up_part = jnp.dot(picked, up_full, preferred_element_type=jnp.float32)
    hidden = (jax.nn.silu(gate_part) * up_part).astype(jnp.bfloat16)
    lower_half = jnp.dot(hidden[:, :FF_HALF], w_down[2 * expert], preferred_element_type=jnp.float32).astype(jnp.bfloat16)
    upper_half = jnp.dot(hidden[:, FF_HALF:], w_down[2 * expert + 1], preferred_element_type=jnp.float32).astype(jnp.bfloat16)
    lower_half, upper_half = lax.optimization_barrier((lower_half, upper_half))
    expert_out = lower_half.astype(jnp.float32) + upper_half.astype(jnp.float32)
    return row_index, gate_row[:, None] * expert_out


def reference(tokens, expert_ids, gate_weights, w_gate, w_up, w_down):
    def per_node(node_index, running):
        node_share = jnp.zeros((TOKENS, D), jnp.float32)
        for slot_index in range(EXP_NODE):
            expert = node_index * EXP_NODE + slot_index
            row_index, gated_term = expert_rows(expert, tokens, expert_ids, gate_weights, w_gate, w_up, w_down)
            node_share = node_share.at[row_index].add(gated_term)
        rounded = lax.optimization_barrier(node_share.astype(jnp.bfloat16))
        return running + rounded.astype(jnp.float32)

    running = lax.fori_loop(0, N_NODE, per_node, jnp.zeros((TOKENS, D), jnp.float32))
    return running.astype(jnp.bfloat16)
```

```python
import functools

import jax
import jax.numpy as jnp
from jax import lax
from jax.experimental import pallas as pl
from jax.experimental.pallas import tpu as pltpu
from jax.sharding import PartitionSpec as P

SLOTS = 5
EXPERTS = 4
NODE_ROWS = EXPERTS * SLOTS // 2
PIECES = 7
NODE_BLOCK = 72
GROUP = 8
GROUP_ROWS = GROUP * NODE_BLOCK
CHUNKS = ((0, 256), (1792, 256))
BF = jnp.bfloat16
F32 = jnp.float32
VMEM = 56 << 20


def dot(a, b):
    return jnp.dot(a, b, preferred_element_type=F32)


def iota(shape, dim):
    return lax.broadcasted_iota(jnp.int32, shape, dim)


def steps(value, step, count):
    total = jnp.zeros_like(value)
    for i in range(1, count):
        total = total + jnp.where(value >= step * i, 1, 0)
    return total


def ones_where(mask):
    return jnp.where(mask, 1.0, 0.0).astype(F32)


def block_position(shape, dim):
    index = iota(shape, dim)
    node = steps(index, NODE_BLOCK, GROUP)
    inner = index - NODE_BLOCK * node
    piece = steps(inner, NODE_ROWS, PIECES + 1)
    return node, piece, inner - NODE_ROWS * piece


def call(kernel, out_shape, **kwargs):
    return pl.pallas_call(
        kernel,
        out_shape=out_shape,
        compiler_params=pltpu.CompilerParams(vmem_limit_bytes=VMEM),
        **kwargs,
    )


def node_code(ids, nodes):
    node = iota((nodes, ids.shape[1]), 0)
    hit = jnp.zeros(node.shape, F32)
    for k in range(ids.shape[0]):
        hit = jnp.maximum(hit, ones_where((ids[k : k + 1, :] >> 2) == node))
    tokens = ids.shape[1]
    before = ones_where(iota((tokens, tokens), 0) < iota((tokens, tokens), 1)).astype(BF)
    return jnp.where(hit > 0, dot(hit.astype(BF), before), -1.0)


def row_meta(ids, gates, code):
    top, tokens = ids.shape
    expert = iota((128, tokens), 0)
    hits = [ones_where(ids[k : k + 1, :] == expert) for k in range(top)]
    before = ones_where(iota((tokens, tokens), 0) < iota((tokens, tokens), 1)).astype(BF)
    rank = dot(functools.reduce(jnp.maximum, hits).astype(BF), before)
    items = [(ids[k : k + 1, :] + 1).astype(F32) for k in range(top)]
    items += [jnp.sum(hits[k] * rank, axis=0, keepdims=True) for k in range(top)]
    items += [gates[k : k + 1, :] for k in range(top)]
    table = jnp.concatenate(
        [jnp.broadcast_to(item, (16, tokens)) for item in items]
        + [jnp.zeros((256 - 16 * len(items), tokens), F32)],
        axis=0,
    )
    place = iota(table.shape, 0) & 15
    meta = jnp.zeros((code.shape[0], 256), F32)
    for r in range(NODE_ROWS):
        meta += lax.dot_general(
            ones_where(code == float(r)).astype(BF),
            jnp.where(place == r, table, 0.0).astype(BF),
            (((1,), (1,)), ((), ())),
            preferred_element_type=F32,
        )
    return meta.astype(BF)


def pack_kernel(with_meta, piece_width, ids_ref, gates_ref, tok_ref, out_ref):
    ids = ids_ref[...]
    nodes = out_ref.shape[0] // NODE_BLOCK
    tokens = ids.shape[1]
    code = node_code(ids, nodes)
    inner = iota((NODE_BLOCK, tokens), 0)
    piece = steps(inner, NODE_ROWS, PIECES + 1)
    row = (inner - NODE_ROWS * piece).astype(F32)
    wanted = [jnp.where(piece == q, row, -9.0) for q in range(PIECES)]
    stacked = jnp.concatenate(
        [tok_ref[:, q * piece_width : (q + 1) * piece_width] for q in range(PIECES)], axis=0
    )
    if with_meta:
        meta = row_meta(ids, gates_ref[...].astype(F32), code)
        node_of, inner_of = steps(iota((GROUP_ROWS, nodes), 0), NODE_BLOCK, GROUP), None
        inner_of = iota((GROUP_ROWS, nodes), 0) - NODE_BLOCK * node_of
    for g in range(nodes // GROUP):
        picks = []
        for q in range(PIECES):
            picks.append(
                jnp.concatenate(
                    [ones_where(code[n : n + 1, :] == wanted[q]) for n in range(g * GROUP, (g + 1) * GROUP)],
                    axis=0,
                ).astype(BF)
            )
        rows = dot(jnp.concatenate(picks, axis=1), stacked)
        if with_meta:
            spot = (node_of + g * GROUP == iota((GROUP_ROWS, nodes), 1)) & (inner_of == PIECES * NODE_ROWS)
            rows += dot(ones_where(spot).astype(BF), meta)
        out_ref[g * GROUP_ROWS : (g + 1) * GROUP_ROWS, :] = rows.astype(BF)


def pack(ids_t, gates_t, tokens, nodes, chunk, with_meta):
    start, width = chunk
    span = PIECES * width
    return call(
        functools.partial(pack_kernel, with_meta, width),
        jax.ShapeDtypeStruct((nodes * NODE_BLOCK, width), BF),
        grid=(1,),
        in_specs=[
            pl.BlockSpec(ids_t.shape, lambda i: (0, 0)),
            pl.BlockSpec(gates_t.shape, lambda i: (0, 0)),
            pl.BlockSpec((tokens.shape[0], span), lambda i: (0, start // span)),
        ],
        out_specs=pl.BlockSpec((nodes * NODE_BLOCK, width), lambda i: (0, 0)),
        name="pack_rows",
    )(ids_t, gates_t, tokens)


def expert_lanes(meta, expert, spread):
    ids = meta[:, :128]
    hit = ones_where(ids == (expert + 1).astype(F32))
    slot = dot((hit * (pltpu.roll(ids, 64, 1) + 1.0)).astype(BF), spread)
    gate = dot((hit * meta[:, 128:256]).astype(BF), spread)
    return slot, gate


def own_lane(values, node, g):
    part = values[g * GROUP : (g + 1) * GROUP, :]
    return jnp.sum(jnp.where(iota(part.shape, 0) == node, part, 0.0), axis=0, keepdims=True)


def lane_tables():
    node, piece, row = block_position((1, GROUP_ROWS), 1)
    lane = iota((128, GROUP_ROWS), 0)
    spread = ones_where(((lane & 15) == row) & (lane < 64)).astype(BF)
    return node, piece, spread


def row_target():
    row = iota((GROUP * SLOTS, GROUP_ROWS), 0)
    node = steps(row, SLOTS, GROUP)
    return (row + (8 - SLOTS) * node + 1).astype(F32)


def select_kernel(with_meta, where_ref, rows_ref, meta_in_ref, *out_refs):
    nodes = rows_ref.shape[0] // NODE_BLOCK
    width = rows_ref.shape[1]
    if with_meta:
        meta_ref, out_refs = out_refs[0], out_refs[1:]
        spot = iota((nodes, rows_ref.shape[0]), 1) == iota((nodes, rows_ref.shape[0]), 0) * NODE_BLOCK + PIECES * NODE_ROWS
        meta = dot(ones_where(spot).astype(BF), rows_ref[...])
        meta_ref[...] = meta
    else:
        meta = meta_in_ref[...]
    node, piece, spread = lane_tables()
    target = row_target()
    slots = []
    for d in range(EXPERTS):
        expert = where_ref[0] * EXPERTS + ((where_ref[1] + d) & (EXPERTS - 1))
        slots.append(expert_lanes(meta, expert, spread)[0])
    shift = 8.0 * node.astype(F32)
    held = [[None] * EXPERTS for _ in range(PIECES)]
    for g in range(nodes // GROUP):
        lines = [own_lane(slots[d], node, g) + shift for d in range(EXPERTS)]
        picks = []
        for q in range(PIECES):
            for d in range(EXPERTS):
                line = jnp.where(piece == q, lines[d], -9.0)
                picks.append(ones_where(target == line))
        picked = dot(
            jnp.concatenate(picks, axis=0).astype(BF), rows_ref[g * GROUP_ROWS : (g + 1) * GROUP_ROWS, :]
        )
        height = GROUP * SLOTS
        for q in range(PIECES):
            for d in range(EXPERTS):
                at = (q * EXPERTS + d) * height
                part = picked[at : at + height]
                if g % 2 == 0:
                    held[q][d] = part
                else:
                    both = jnp.concatenate([held[q][d], part], axis=0).astype(BF)
                    out_refs[d][(g - 1) * height : (g + 1) * height, q * width : (q + 1) * width] = both


def select(where, rows, meta, nodes):
    width = rows.shape[1]
    with_meta = meta is None
    shapes = [jax.ShapeDtypeStruct((nodes * SLOTS, PIECES * width), BF)] * EXPERTS
    if with_meta:
        shapes = [jax.ShapeDtypeStruct((nodes, 256), F32)] + shapes
        meta = jnp.zeros((8, 256), F32)
    out = call(
        functools.partial(select_kernel, with_meta),
        shapes,
        in_specs=[
            pl.BlockSpec(memory_space=pltpu.SMEM),
            pl.BlockSpec(memory_space=pltpu.VMEM),
            pl.BlockSpec(memory_space=pltpu.VMEM),
        ],
        name="select_rows",
    )(where, rows, meta)
    return (out[0], out[1:]) if with_meta else (None, out)


def mix_kernel(where_ref, meta_ref, *refs):
    out_ref, value_refs = refs[-1], refs[:-1]
    nodes = out_ref.shape[0] // NODE_BLOCK
    width = out_ref.shape[1]
    meta = meta_ref[...]
    node, _, spread = lane_tables()
    target = row_target()
    tables = []
    for d in range(EXPERTS):
        expert = where_ref[0] * EXPERTS + ((where_ref[1] + d) & (EXPERTS - 1))
        tables.append(expert_lanes(meta, expert, spread))
    shift = 8.0 * node.astype(F32)
    _, out_piece, _ = block_position((GROUP_ROWS, width), 0)
    height = GROUP * SLOTS
    for g in range(nodes // GROUP):
        gated = []
        values = []
        for d in range(EXPERTS):
            line = own_lane(tables[d][0], node, g) + shift
            gate = own_lane(tables[d][1], node, g)
            gated.append(jnp.where(target == line, jnp.broadcast_to(gate, target.shape), 0.0))
            pair = value_refs[d][(g // 2) * 2 * height : (g // 2 + 1) * 2 * height, :].astype(F32)
            values.append(pair[(g % 2) * height : (g % 2 + 1) * height, :])
        share = lax.dot_general(
            jnp.concatenate(gated, axis=0).astype(BF),
            jnp.concatenate(values, axis=0).astype(BF),
            (((0,), (0,)), ((), ())),
            preferred_element_type=F32,
        )
        total = jnp.zeros((GROUP_ROWS, width), F32)
        for q in range(PIECES):
            total = jnp.where(out_piece == q, share[:, q * width : (q + 1) * width], total)
        out_ref[g * GROUP_ROWS : (g + 1) * GROUP_ROWS, :] = total.astype(BF)


def mix(where, meta, values, nodes):
    width = values[0].shape[1] // PIECES
    return call(
        mix_kernel,
        jax.ShapeDtypeStruct((nodes * NODE_BLOCK, width), BF),
        in_specs=[pl.BlockSpec(memory_space=pltpu.SMEM)]
        + [pl.BlockSpec(memory_space=pltpu.VMEM)] * (1 + len(values)),
        name="node_share",
    )(where, meta, *values)


def finish_kernel(width, ids_ref, home_ref, *refs):
    out_ref = refs[-1]
    tokens, top = ids_ref.shape
    nodes = home_ref.shape[0] // NODE_BLOCK
    node = iota((tokens, nodes), 1)
    hit = jnp.zeros((tokens, nodes), F32)
    for k in range(top):
        hit = jnp.maximum(hit, ones_where((ids_ref[:, k : k + 1] >> 2) == node))
    before = ones_where(iota((tokens, tokens), 1) < iota((tokens, tokens), 0)).astype(BF)
    code = jnp.where(hit > 0, dot(before, hit.astype(BF)) + 1.0, 0.0).astype(BF)
    lane_node, piece, row = block_position((1, GROUP_ROWS), 1)
    total = jnp.zeros((PIECES * tokens, width), F32)
    for g in range(nodes // GROUP):
        spread = ones_where(iota((nodes, GROUP_ROWS), 0) == lane_node + g * GROUP).astype(BF)
        lanes = dot(code, spread)
        picks = []
        for q in range(PIECES):
            line = jnp.where(piece == q, row + 1, -9).astype(F32)
            picks.append(ones_where(lanes == line))
        total += dot(
            jnp.concatenate(picks, axis=0).astype(BF), home_ref[g * GROUP_ROWS : (g + 1) * GROUP_ROWS, :]
        )
    for q in range(PIECES):
        out_ref[:, q * width : (q + 1) * width] = total[q * tokens : (q + 1) * tokens, :].astype(BF)


def finish(ids, home, chunk, before, columns):
    start, width = chunk
    span = PIECES * width
    specs = [
        pl.BlockSpec(ids.shape, lambda i: (0, 0)),
        pl.BlockSpec(home.shape, lambda i: (0, 0)),
    ]
    args = [ids, home]
    aliases = {}
    if before is not None:
        specs.append(pl.BlockSpec(memory_space=pl.ANY))
        args.append(before)
        aliases = {2: 0}
    return call(
        functools.partial(finish_kernel, width),
        jax.ShapeDtypeStruct((ids.shape[0], columns), BF),
        grid=(1,),
        in_specs=specs,
        out_specs=pl.BlockSpec((ids.shape[0], span), lambda i: (0, start // span)),
        input_output_aliases=aliases,
        name="sum_over_nodes",
    )(*args)


def up_kernel(first, last, *refs):
    (own_ref, other_ref, gate_ref, up_ref), refs = refs[:4], refs[4:]
    if not first:
        (gate_in_ref, up_in_ref), refs = refs[:2], refs[2:]
    outs, (gate_acc, up_acc) = refs[:-2], refs[-2:]
    step = pl.program_id(0)
    rows = own_ref.shape[0]
    for index, x_ref in enumerate((own_ref, other_ref)):
        at = slice(index * rows, (index + 1) * rows)
        for w_ref, acc, source in ((gate_ref, gate_acc, 0), (up_ref, up_acc, 1)):
            part = dot(x_ref[...], w_ref[0])

            @pl.when(step == 0)
            def _(acc=acc, part=part, at=at, source=source):
                if first:
                    acc[at, :] = part
                else:
                    acc[at, :] = (gate_in_ref, up_in_ref)[source][at, :] + part

            @pl.when(step > 0)
            def _(acc=acc, part=part, at=at):
                acc[at, :] += part

    @pl.when(step == pl.num_programs(0) - 1)
    def _():
        if last:
            gate = gate_acc[...]
            outs[0][...] = ((gate / (1.0 + jnp.exp(-gate))) * up_acc[...]).astype(BF)
        else:
            outs[0][...] = gate_acc[...]
            outs[1][...] = up_acc[...]


def up_step(own, other, w_gate, w_up, chunk, sums, last):
    start, width = chunk
    span = PIECES * width
    depth = 896
    base = start // depth
    rows = own.shape[0]
    units = w_gate.shape[2]
    first = sums is None
    whole = pl.BlockSpec((2 * rows, units), lambda i: (0, 0))
    x_spec = pl.BlockSpec((rows, depth), lambda i: (0, i))
    w_spec = pl.BlockSpec((1, depth, units), lambda i: (0, base + i, 0))
    shape = (
        jax.ShapeDtypeStruct((2 * rows, units), BF)
        if last
        else [jax.ShapeDtypeStruct((2 * rows, units), F32)] * 2
    )
    return call(
        functools.partial(up_kernel, first, last),
        shape,
        grid=(span // depth,),
        in_specs=[x_spec, x_spec, w_spec, w_spec] + ([] if first else [whole, whole]),
        out_specs=whole if last else [whole, whole],
        scratch_shapes=[pltpu.VMEM((2 * rows, units), F32)] * 2,
        name="gate_up",
    )(own, other, w_gate, w_up, *(() if first else sums))


def down_other_kernel(hidden_ref, w_ref, out_ref):
    out_ref[...] = dot(hidden_ref[...], w_ref[0]).astype(BF)


def down_own_kernel(hidden_ref, w_ref, mate_ref, *out_refs):
    mine = dot(hidden_ref[...], w_ref[0]).astype(BF)
    value = (mine.astype(F32) + mate_ref[...].astype(F32)).astype(BF)
    rows = out_refs[0].shape[0]
    for d, out_ref in enumerate(out_refs):
        out_ref[...] = value[d * rows : (d + 1) * rows, :]


def down_other(hidden, w_down, chunk):
    start, width = chunk
    span = PIECES * width
    tile = 896
    rows, units = hidden.shape[0] // 2, hidden.shape[1]
    return call(
        down_other_kernel,
        jax.ShapeDtypeStruct((rows, span), BF),
        grid=(span // tile,),
        in_specs=[
            pl.BlockSpec((rows, units), lambda i: (1, 0)),
            pl.BlockSpec((1, units, tile), lambda i: (0, 0, start // tile + i)),
        ],
        out_specs=pl.BlockSpec((rows, tile), lambda i: (0, i)),
        name="down_other",
    )(hidden, w_down)


def down_own(hidden, w_down, mate, chunk):
    start, width = chunk
    span = PIECES * width
    tile = 896
    rows, units = hidden.shape[0] // 2, hidden.shape[1]
    part = rows // EXPERTS
    return call(
        down_own_kernel,
        [jax.ShapeDtypeStruct((part, span), BF)] * EXPERTS,
        grid=(span // tile,),
        in_specs=[
            pl.BlockSpec((rows, units), lambda i: (0, 0)),
            pl.BlockSpec((1, units, tile), lambda i: (0, 0, start // tile + i)),
            pl.BlockSpec((rows, tile), lambda i: (0, i)),
        ],
        out_specs=[pl.BlockSpec((part, tile), lambda i: (0, i))] * EXPERTS,
        name="down_own",
    )(hidden, w_down, mate)


def over_nodes(rows, nodes):
    cut = rows.reshape(nodes, NODE_BLOCK, rows.shape[1])
    return lax.all_to_all(cut, "node", split_axis=0, concat_axis=0, tiled=True).reshape(rows.shape)


def along_y(block, distance):
    pairs = [(y * 2 + c, ((y + distance) % EXPERTS) * 2 + c) for y in range(EXPERTS) for c in range(2)]
    return lax.ppermute(block, "local", pairs)


def to_mate(block):
    return lax.ppermute(block, "local", [(i, i ^ 1) for i in range(2 * EXPERTS)])


def per_device(tokens, expert_ids, gate_weights, w_gate, w_up, w_down):
    nodes = lax.axis_size("node")
    columns = tokens.shape[1]
    where = jnp.stack([lax.axis_index("node"), lax.axis_index("local") // 2]).astype(jnp.int32)
    ids_t = expert_ids.T
    gates_t = gate_weights.T
    meta = None
    sums = None
    packed = [pack(ids_t, gates_t, tokens, nodes, chunk, i == 0) for i, chunk in enumerate(CHUNKS)]
    arrived = [over_nodes(rows, nodes) for rows in packed]
    for i, chunk in enumerate(CHUNKS):
        got, blocks = select(where, arrived[i], meta, nodes)
        meta = got if meta is None else meta
        own = jnp.concatenate([blocks[0]] + [along_y(blocks[d], d) for d in range(1, EXPERTS)], axis=0)
        other = to_mate(own)
        sums = up_step(own, other, w_gate, w_up, chunk, sums, i == len(CHUNKS) - 1)
    hidden = sums
    mates = [to_mate(down_other(hidden, w_down, chunk)) for chunk in CHUNKS]
    mixed = None
    for i, chunk in enumerate(CHUNKS):
        values = down_own(hidden, w_down, mates[i], chunk)
        values = [values[0]] + [along_y(values[d], -d) for d in range(1, EXPERTS)]
        home = over_nodes(mix(where, meta, values, nodes), nodes)
        mixed = finish(expert_ids, home, chunk, mixed, columns)
    return mixed


def solution(mesh):
    rows = P(("node", "local"), None)
    cube = P(("node", "local"), None, None)
    return jax.shard_map(
        per_device,
        mesh=mesh,
        in_specs=(rows, rows, rows, cube, cube, cube),
        out_specs=rows,
        check_vma=False,
    )
```

```python
import functools

import jax
import jax.numpy as jnp
from jax import lax
from jax.experimental import pallas as pl
from jax.experimental.pallas import tpu as pltpu
from jax.sharding import PartitionSpec as P

SLOTS = 5
EXPERTS = 4
NODE_ROWS = EXPERTS * SLOTS // 2
PIECES = 7
NODE_BLOCK = 72
GROUP = 8
GROUP_ROWS = GROUP * NODE_BLOCK
CHUNKS = ((0, 256), (1792, 256))
BF = jnp.bfloat16
F32 = jnp.float32
VMEM = 56 << 20


def dot(a, b):
    return jnp.dot(a, b, preferred_element_type=F32)


def iota(shape, dim):
    return lax.broadcasted_iota(jnp.int32, shape, dim)


def steps(value, step, count):
    total = jnp.zeros_like(value)
    for i in range(1, count):
        total = total + jnp.where(value >= step * i, 1, 0)
    return total


def ones_where(mask):
    return jnp.where(mask, 1.0, 0.0).astype(F32)


def block_position(shape, dim):
    index = iota(shape, dim)
    node = steps(index, NODE_BLOCK, GROUP)
    inner = index - NODE_BLOCK * node
    piece = steps(inner, NODE_ROWS, PIECES + 1)
    return node, piece, inner - NODE_ROWS * piece


def call(kernel, out_shape, cost, **kwargs):
    return pl.pallas_call(
        kernel,
        out_shape=out_shape,
        cost_estimate=pl.CostEstimate(flops=cost * 10**9, bytes_accessed=10**6, transcendentals=0),
        compiler_params=pltpu.CompilerParams(vmem_limit_bytes=VMEM),
        **kwargs,
    )


def node_code(ids, nodes):
    node = iota((nodes, ids.shape[1]), 0)
    hit = jnp.zeros(node.shape, F32)
    for k in range(ids.shape[0]):
        hit = jnp.maximum(hit, ones_where((ids[k : k + 1, :] >> 2) == node))
    tokens = ids.shape[1]
    before = ones_where(iota((tokens, tokens), 0) < iota((tokens, tokens), 1)).astype(BF)
    return jnp.where(hit > 0, dot(hit.astype(BF), before), -1.0)


def row_meta(ids, gates, code):
    top, tokens = ids.shape
    expert = iota((128, tokens), 0)
    hits = [ones_where(ids[k : k + 1, :] == expert) for k in range(top)]
    before = ones_where(iota((tokens, tokens), 0) < iota((tokens, tokens), 1)).astype(BF)
    rank = dot(functools.reduce(jnp.maximum, hits).astype(BF), before)
    items = [(ids[k : k + 1, :] + 1).astype(F32) for k in range(top)]
    items += [jnp.sum(hits[k] * rank, axis=0, keepdims=True) for k in range(top)]
    items += [gates[k : k + 1, :] for k in range(top)]
    table = jnp.concatenate(
        [jnp.broadcast_to(item, (16, tokens)) for item in items]
        + [jnp.zeros((256 - 16 * len(items), tokens), F32)],
        axis=0,
    )
    place = iota(table.shape, 0) & 15
    meta = jnp.zeros((code.shape[0], 256), F32)
    for r in range(NODE_ROWS):
        meta += lax.dot_general(
            ones_where(code == float(r)).astype(BF),
            jnp.where(place == r, table, 0.0).astype(BF),
            (((1,), (1,)), ((), ())),
            preferred_element_type=F32,
        )
    return meta.astype(BF)


def pack_kernel(with_meta, piece_width, ids_ref, gates_ref, tok_ref, out_ref):
    ids = ids_ref[...]
    nodes = out_ref.shape[0] // NODE_BLOCK
    tokens = ids.shape[1]
    code = node_code(ids, nodes)
    inner = iota((NODE_BLOCK, tokens), 0)
    piece = steps(inner, NODE_ROWS, PIECES + 1)
    row = (inner - NODE_ROWS * piece).astype(F32)
    wanted = [jnp.where(piece == q, row, -9.0) for q in range(PIECES)]
    stacked = jnp.concatenate(
        [tok_ref[:, q * piece_width : (q + 1) * piece_width] for q in range(PIECES)], axis=0
    )
    if with_meta:
        meta = row_meta(ids, gates_ref[...].astype(F32), code)
        node_of, inner_of = steps(iota((GROUP_ROWS, nodes), 0), NODE_BLOCK, GROUP), None
        inner_of = iota((GROUP_ROWS, nodes), 0) - NODE_BLOCK * node_of
    for g in range(nodes // GROUP):
        picks = []
        for q in range(PIECES):
            picks.append(
                jnp.concatenate(
                    [ones_where(code[n : n + 1, :] == wanted[q]) for n in range(g * GROUP, (g + 1) * GROUP)],
                    axis=0,
                ).astype(BF)
            )
        rows = dot(jnp.concatenate(picks, axis=1), stacked)
        if with_meta:
            spot = (node_of + g * GROUP == iota((GROUP_ROWS, nodes), 1)) & (inner_of == PIECES * NODE_ROWS)
            rows += dot(ones_where(spot).astype(BF), meta)
        out_ref[g * GROUP_ROWS : (g + 1) * GROUP_ROWS, :] = rows.astype(BF)


def pack(ids_t, gates_t, tokens, nodes, chunk, with_meta):
    start, width = chunk
    span = PIECES * width
    return call(
        functools.partial(pack_kernel, with_meta, width),
        jax.ShapeDtypeStruct((nodes * NODE_BLOCK, width), BF),
        grid=(1,),
        in_specs=[
            pl.BlockSpec(ids_t.shape, lambda i: (0, 0)),
            pl.BlockSpec(gates_t.shape, lambda i: (0, 0)),
            pl.BlockSpec((tokens.shape[0], span), lambda i: (0, start // span)),
        ],
        out_specs=pl.BlockSpec((nodes * NODE_BLOCK, width), lambda i: (0, 0)),
        cost=5,
        name="pack_rows",
    )(ids_t, gates_t, tokens)


def expert_lanes(meta, expert, spread):
    ids = meta[:, :128]
    hit = ones_where(ids == (expert + 1).astype(F32))
    slot = dot((hit * (pltpu.roll(ids, 64, 1) + 1.0)).astype(BF), spread)
    gate = dot((hit * meta[:, 128:256]).astype(BF), spread)
    return slot, gate


def own_lane(values, node, g):
    part = values[g * GROUP : (g + 1) * GROUP, :]
    return jnp.sum(jnp.where(iota(part.shape, 0) == node, part, 0.0), axis=0, keepdims=True)


def lane_tables():
    node, piece, row = block_position((1, GROUP_ROWS), 1)
    lane = iota((128, GROUP_ROWS), 0)
    spread = ones_where(((lane & 15) == row) & (lane < 64)).astype(BF)
    return node, piece, spread


def row_target():
    row = iota((GROUP * SLOTS, GROUP_ROWS), 0)
    node = steps(row, SLOTS, GROUP)
    return (row + (8 - SLOTS) * node + 1).astype(F32)


def select_kernel(with_meta, where_ref, rows_ref, meta_in_ref, *out_refs):
    nodes = rows_ref.shape[0] // NODE_BLOCK
    width = rows_ref.shape[1]
    if with_meta:
        meta_ref, out_refs = out_refs[0], out_refs[1:]
        spot = iota((nodes, rows_ref.shape[0]), 1) == iota((nodes, rows_ref.shape[0]), 0) * NODE_BLOCK + PIECES * NODE_ROWS
        meta = dot(ones_where(spot).astype(BF), rows_ref[...])
        meta_ref[...] = meta
    else:
        meta = meta_in_ref[...]
    node, piece, spread = lane_tables()
    target = row_target()
    slots = []
    for d in range(EXPERTS):
        expert = where_ref[0] * EXPERTS + ((where_ref[1] + d) & (EXPERTS - 1))
        slots.append(expert_lanes(meta, expert, spread)[0])
    shift = 8.0 * node.astype(F32)
    held = [[None] * EXPERTS for _ in range(PIECES)]
    for g in range(nodes // GROUP):
        lines = [own_lane(slots[d], node, g) + shift for d in range(EXPERTS)]
        picks = []
        for q in range(PIECES):
            for d in range(EXPERTS):
                line = jnp.where(piece == q, lines[d], -9.0)
                picks.append(ones_where(target == line))
        picked = dot(
            jnp.concatenate(picks, axis=0).astype(BF), rows_ref[g * GROUP_ROWS : (g + 1) * GROUP_ROWS, :]
        )
        height = GROUP * SLOTS
        for q in range(PIECES):
            for d in range(EXPERTS):
                at = (q * EXPERTS + d) * height
                part = picked[at : at + height]
                if g % 2 == 0:
                    held[q][d] = part
                else:
                    both = jnp.concatenate([held[q][d], part], axis=0).astype(BF)
                    out_refs[d][(g - 1) * height : (g + 1) * height, q * width : (q + 1) * width] = both


def select(where, rows, meta, nodes):
    width = rows.shape[1]
    with_meta = meta is None
    shapes = [jax.ShapeDtypeStruct((nodes * SLOTS, PIECES * width), BF)] * EXPERTS
    if with_meta:
        shapes = [jax.ShapeDtypeStruct((nodes, 256), F32)] + shapes
        meta = jnp.zeros((8, 256), F32)
    out = call(
        functools.partial(select_kernel, with_meta),
        shapes,
        in_specs=[
            pl.BlockSpec(memory_space=pltpu.SMEM),
            pl.BlockSpec(memory_space=pltpu.VMEM),
            pl.BlockSpec(memory_space=pltpu.VMEM),
        ],
        cost=20,
        name="select_rows",
    )(where, rows, meta)
    return (out[0], out[1:]) if with_meta else (None, out)


def mix_kernel(where_ref, meta_ref, *refs):
    out_ref, value_refs = refs[-1], refs[:-1]
    nodes = out_ref.shape[0] // NODE_BLOCK
    width = out_ref.shape[1]
    meta = meta_ref[...]
    node, _, spread = lane_tables()
    target = row_target()
    tables = []
    for d in range(EXPERTS):
        expert = where_ref[0] * EXPERTS + ((where_ref[1] + d) & (EXPERTS - 1))
        tables.append(expert_lanes(meta, expert, spread))
    shift = 8.0 * node.astype(F32)
    _, out_piece, _ = block_position((GROUP_ROWS, width), 0)
    height = GROUP * SLOTS
    for g in range(nodes // GROUP):
        gated = []
        values = []
        for d in range(EXPERTS):
            line = own_lane(tables[d][0], node, g) + shift
            gate = own_lane(tables[d][1], node, g)
            gated.append(jnp.where(target == line, jnp.broadcast_to(gate, target.shape), 0.0))
            pair = value_refs[d][(g // 2) * 2 * height : (g // 2 + 1) * 2 * height, :].astype(F32)
            values.append(pair[(g % 2) * height : (g % 2 + 1) * height, :])
        share = lax.dot_general(
            jnp.concatenate(gated, axis=0).astype(BF),
            jnp.concatenate(values, axis=0).astype(BF),
            (((0,), (0,)), ((), ())),
            preferred_element_type=F32,
        )
        total = jnp.zeros((GROUP_ROWS, width), F32)
        for q in range(PIECES):
            total = jnp.where(out_piece == q, share[:, q * width : (q + 1) * width], total)
        out_ref[g * GROUP_ROWS : (g + 1) * GROUP_ROWS, :] = total.astype(BF)


def mix(where, meta, values, nodes):
    width = values[0].shape[1] // PIECES
    return call(
        mix_kernel,
        jax.ShapeDtypeStruct((nodes * NODE_BLOCK, width), BF),
        in_specs=[pl.BlockSpec(memory_space=pltpu.SMEM)]
        + [pl.BlockSpec(memory_space=pltpu.VMEM)] * (1 + len(values)),
        cost=40,
        name="node_share",
    )(where, meta, *values)


def finish_kernel(width, ids_ref, home_ref, *refs):
    out_ref = refs[-1]
    tokens, top = ids_ref.shape
    nodes = home_ref.shape[0] // NODE_BLOCK
    node = iota((tokens, nodes), 1)
    hit = jnp.zeros((tokens, nodes), F32)
    for k in range(top):
        hit = jnp.maximum(hit, ones_where((ids_ref[:, k : k + 1] >> 2) == node))
    before = ones_where(iota((tokens, tokens), 1) < iota((tokens, tokens), 0)).astype(BF)
    code = jnp.where(hit > 0, dot(before, hit.astype(BF)) + 1.0, 0.0).astype(BF)
    lane_node, piece, row = block_position((1, GROUP_ROWS), 1)
    total = jnp.zeros((PIECES * tokens, width), F32)
    for g in range(nodes // GROUP):
        spread = ones_where(iota((nodes, GROUP_ROWS), 0) == lane_node + g * GROUP).astype(BF)
        lanes = dot(code, spread)
        picks = []
        for q in range(PIECES):
            line = jnp.where(piece == q, row + 1, -9).astype(F32)
            picks.append(ones_where(lanes == line))
        total += dot(
            jnp.concatenate(picks, axis=0).astype(BF), home_ref[g * GROUP_ROWS : (g + 1) * GROUP_ROWS, :]
        )
    for q in range(PIECES):
        out_ref[:, q * width : (q + 1) * width] = total[q * tokens : (q + 1) * tokens, :].astype(BF)


def finish(ids, home, chunk, before, columns):
    start, width = chunk
    span = PIECES * width
    specs = [
        pl.BlockSpec(ids.shape, lambda i: (0, 0)),
        pl.BlockSpec(home.shape, lambda i: (0, 0)),
    ]
    args = [ids, home]
    aliases = {}
    if before is not None:
        specs.append(pl.BlockSpec(memory_space=pl.ANY))
        args.append(before)
        aliases = {2: 0}
    return call(
        functools.partial(finish_kernel, width),
        jax.ShapeDtypeStruct((ids.shape[0], columns), BF),
        grid=(1,),
        in_specs=specs,
        out_specs=pl.BlockSpec((ids.shape[0], span), lambda i: (0, start // span)),
        input_output_aliases=aliases,
        cost=6,
        name="sum_over_nodes",
    )(*args)


def up_kernel(start, down_start, *refs):
    last = down_start is not None
    count = 2 * EXPERTS
    blocks, (gate_ref, up_ref), refs = refs[:count], refs[count : count + 2], refs[count + 2 :]
    if last:
        sums_in, down_ref, refs = refs[:2], refs[2], refs[3:]
        (hidden_ref, other_out), (x_ref, wg_ref, wu_ref, *sums, wd_ref, other_ref, sems) = refs[:2], refs[2:]
    else:
        outs, (x_ref, wg_ref, wu_ref, sems) = refs[:2], refs[2:]
    rows, span = blocks[0].shape
    band = pl.ds(start, span)
    used = iter(range(64))

    def begin(source, target):
        copy = pltpu.make_async_copy(source, target, sems.at[next(used)])
        copy.start()
        return copy

    weights = [begin(gate_ref.at[0, band, :], wg_ref), begin(up_ref.at[0, band, :], wu_ref)]
    order = [EXPERTS, EXPERTS + 2, 0, 2] if last else [0, 2, EXPERTS, EXPERTS + 2]
    loads = {}
    for i in order:
        at = pl.ds(i * rows, 2 * rows)
        loads[i] = [begin(blocks[k], x_ref.at[pl.ds(k * rows, rows), :]) for k in (i, i + 1)]
        if last:
            loads[i] += [begin(source.at[at, :], target.at[at, :]) for source, target in zip(sums_in, sums)]
            if i == order[1]:
                weights_down = begin(down_ref.at[0, :, pl.ds(down_start, other_ref.shape[1])], wd_ref)
    for copy in weights:
        copy.wait()
    for i in order:
        for copy in loads[i]:
            copy.wait()
        at = pl.ds(i * rows, 2 * rows)
        gate = dot(x_ref[at, :], wg_ref[...])
        up = dot(x_ref[at, :], wu_ref[...])
        if last:
            gate += sums[0][at, :]
            up += sums[1][at, :]
            hidden_ref[at, :] = ((gate / (1.0 + jnp.exp(-gate))) * up).astype(BF)
            if i == order[1]:
                weights_down.wait()
                other_ref[...] = dot(hidden_ref[pl.ds(EXPERTS * rows, EXPERTS * rows), :], wd_ref[...]).astype(BF)
                sent = begin(other_ref, other_out)
        else:
            outs[0][at, :] = gate
            outs[1][at, :] = up
    if last:
        sent.wait()


def up_step(blocks, w_gate, w_up, chunk):
    start, width = chunk
    span = PIECES * width
    rows = blocks[0].shape[0] * len(blocks)
    units = w_gate.shape[2]
    any_spec = pl.BlockSpec(memory_space=pl.ANY)
    args = list(blocks) + [w_gate, w_up]
    return call(
        functools.partial(up_kernel, start, None),
        [jax.ShapeDtypeStruct((rows, units), F32)] * 2,
        in_specs=[any_spec] * len(args),
        scratch_shapes=[
            pltpu.VMEM((rows, span), BF),
            pltpu.VMEM((span, units), BF),
            pltpu.VMEM((span, units), BF),
            pltpu.SemaphoreType.DMA((2 + len(blocks),)),
        ],
        cost=40,
        name="gate_up",
    )(*args)


def hidden_step(blocks, w_gate, w_up, sums, w_down, chunk, down_chunk):
    start, width = chunk
    span, down_span = PIECES * width, PIECES * down_chunk[1]
    rows = blocks[0].shape[0] * len(blocks)
    units = w_gate.shape[2]
    any_spec = pl.BlockSpec(memory_space=pl.ANY)
    args = list(blocks) + [w_gate, w_up] + list(sums) + [w_down]
    return call(
        functools.partial(up_kernel, start, down_chunk[0]),
        [jax.ShapeDtypeStruct((rows, units), BF), jax.ShapeDtypeStruct((rows // 2, down_span), BF)],
        in_specs=[any_spec] * len(args),
        out_specs=[pl.BlockSpec(memory_space=pltpu.VMEM), any_spec],
        scratch_shapes=[
            pltpu.VMEM((rows, span), BF),
            pltpu.VMEM((span, units), BF),
            pltpu.VMEM((span, units), BF),
            pltpu.VMEM((rows, units), F32),
            pltpu.VMEM((rows, units), F32),
            pltpu.VMEM((units, down_span), BF),
            pltpu.VMEM((rows // 2, down_span), BF),
            pltpu.SemaphoreType.DMA((4 + 3 * len(blocks),)),
        ],
        cost=10,
        name="hidden_down",
    )(*args)


def down_other_kernel(hidden_ref, w_ref, out_ref):
    out_ref[...] = dot(hidden_ref[...], w_ref[0]).astype(BF)


def down_own_kernel(hidden_ref, w_ref, mate_ref, *out_refs):
    mine = dot(hidden_ref[...], w_ref[0]).astype(BF)
    value = (mine.astype(F32) + mate_ref[...].astype(F32)).astype(BF)
    rows = out_refs[0].shape[0]
    for d, out_ref in enumerate(out_refs):
        out_ref[...] = value[d * rows : (d + 1) * rows, :]


def down_other(hidden, w_down, chunk):
    start, width = chunk
    span = PIECES * width
    tile = 896
    rows, units = hidden.shape[0] // 2, hidden.shape[1]
    return call(
        down_other_kernel,
        jax.ShapeDtypeStruct((rows, span), BF),
        grid=(span // tile,),
        in_specs=[
            pl.BlockSpec((rows, units), lambda i: (1, 0)),
            pl.BlockSpec((1, units, tile), lambda i: (0, 0, start // tile + i)),
        ],
        out_specs=pl.BlockSpec((rows, tile), lambda i: (0, i)),
        cost=4,
        name="down_other",
    )(hidden, w_down)


def down_own(hidden, w_down, mate, chunk):
    start, width = chunk
    span = PIECES * width
    tile = 896
    rows, units = hidden.shape[0] // 2, hidden.shape[1]
    part = rows // EXPERTS
    return call(
        down_own_kernel,
        [jax.ShapeDtypeStruct((part, span), BF)] * EXPERTS,
        grid=(span // tile,),
        in_specs=[
            pl.BlockSpec((rows, units), lambda i: (0, 0)),
            pl.BlockSpec((1, units, tile), lambda i: (0, 0, start // tile + i)),
            pl.BlockSpec((rows, tile), lambda i: (0, i)),
        ],
        out_specs=[pl.BlockSpec((part, tile), lambda i: (0, i))] * EXPERTS,
        cost=4,
        name="down_own",
    )(hidden, w_down, mate)


def over_nodes(rows, nodes):
    cut = rows.reshape(nodes, NODE_BLOCK, rows.shape[1])
    return lax.all_to_all(cut, "node", split_axis=0, concat_axis=0, tiled=True).reshape(rows.shape)


def along_y(block, distance):
    pairs = [(y * 2 + c, ((y + distance) % EXPERTS) * 2 + c) for y in range(EXPERTS) for c in range(2)]
    return lax.ppermute(block, "local", pairs)


def to_mate(block):
    return lax.ppermute(block, "local", [(i, i ^ 1) for i in range(2 * EXPERTS)])


def per_device(tokens, expert_ids, gate_weights, w_gate, w_up, w_down):
    nodes = lax.axis_size("node")
    columns = tokens.shape[1]
    where = jnp.stack([lax.axis_index("node"), lax.axis_index("local") // 2]).astype(jnp.int32)
    ids_t = expert_ids.T
    gates_t = gate_weights.T
    first, second = CHUNKS
    packed = [pack(ids_t, gates_t, tokens, nodes, chunk, chunk is first) for chunk in CHUNKS]
    arrived = [over_nodes(rows, nodes) for rows in packed]
    meta, blocks = select(where, arrived[0], None, nodes)
    own = [blocks[0]] + [along_y(blocks[d], d) for d in range(1, EXPERTS)]
    near = to_mate(blocks[0])
    _, blocks = select(where, arrived[1], meta, nodes)
    own, near, blocks = lax.optimization_barrier((own, near, blocks))
    later = [along_y(blocks[d], d) for d in range(1, EXPERTS)]
    later_near = to_mate(blocks[0])
    sums = up_step(own + [near] + [to_mate(block) for block in own[1:]], w_gate, w_up, first)
    later, sums = lax.optimization_barrier((later, sums))
    own = [blocks[0]] + later
    hidden, other = hidden_step(
        own + [later_near] + [to_mate(block) for block in later], w_gate, w_up, sums, w_down, second, first
    )
    mate = to_mate(other)
    later_mate = to_mate(down_other(hidden, w_down, second))
    values = down_own(hidden, w_down, mate, first)
    back = [values[0]] + [along_y(values[d], -d) for d in range(1, EXPERTS)]
    values = down_own(hidden, w_down, later_mate, second)
    back, values = lax.optimization_barrier((back, values))
    later_back = [values[0]] + [along_y(values[d], -d) for d in range(1, EXPERTS)]
    mixed = None
    for chunk, rows in ((first, back), (second, later_back)):
        home = over_nodes(mix(where, meta, rows, nodes), nodes)
        mixed = finish(expert_ids, home, chunk, mixed, columns)
    return mixed


def solution(mesh):
    rows = P(("node", "local"), None)
    cube = P(("node", "local"), None, None)
    return jax.shard_map(
        per_device,
        mesh=mesh,
        in_specs=(rows, rows, rows, cube, cube, cube),
        out_specs=rows,
        check_vma=False,
    )
```

```python
import functools

import jax
import jax.numpy as jnp
from jax import lax
from jax.experimental import pallas as pl
from jax.experimental.pallas import tpu as pltpu
from jax.sharding import PartitionSpec as P

SLOTS = 5
EXPERTS = 4
NODE_ROWS = EXPERTS * SLOTS // 2
PIECES = 7
NODE_BLOCK = 72
GROUP = 8
GROUP_ROWS = GROUP * NODE_BLOCK
CHUNKS = ((0, 256), (1792, 256))
BF = jnp.bfloat16
F32 = jnp.float32
VMEM = 63 << 20


def dot(a, b):
    return jnp.dot(a, b, preferred_element_type=F32)


def iota(shape, dim):
    return lax.broadcasted_iota(jnp.int32, shape, dim)


def steps(value, step, count):
    total = jnp.zeros_like(value)
    for i in range(1, count):
        total = total + jnp.where(value >= step * i, 1, 0)
    return total


def ones_where(mask):
    return jnp.where(mask, 1.0, 0.0).astype(F32)


def block_position(shape, dim):
    index = iota(shape, dim)
    node = steps(index, NODE_BLOCK, GROUP)
    inner = index - NODE_BLOCK * node
    piece = steps(inner, NODE_ROWS, PIECES + 1)
    return node, piece, inner - NODE_ROWS * piece


def call(kernel, out_shape, cost, **kwargs):
    return pl.pallas_call(
        kernel,
        out_shape=out_shape,
        cost_estimate=pl.CostEstimate(flops=cost * 10**9, bytes_accessed=10**6, transcendentals=0),
        compiler_params=pltpu.CompilerParams(vmem_limit_bytes=VMEM),
        **kwargs,
    )


def node_code(ids, nodes):
    node = iota((nodes, ids.shape[1]), 0)
    hit = jnp.zeros(node.shape, F32)
    for k in range(ids.shape[0]):
        hit = jnp.maximum(hit, ones_where((ids[k : k + 1, :] >> 2) == node))
    tokens = ids.shape[1]
    before = ones_where(iota((tokens, tokens), 0) < iota((tokens, tokens), 1)).astype(BF)
    return jnp.where(hit > 0, dot(hit.astype(BF), before), -1.0)


def row_meta(ids, gates, code):
    top, tokens = ids.shape
    expert = iota((128, tokens), 0)
    hits = [ones_where(ids[k : k + 1, :] == expert) for k in range(top)]
    before = ones_where(iota((tokens, tokens), 0) < iota((tokens, tokens), 1)).astype(BF)
    rank = dot(functools.reduce(jnp.maximum, hits).astype(BF), before)
    items = [(ids[k : k + 1, :] + 1).astype(F32) for k in range(top)]
    items += [jnp.sum(hits[k] * rank, axis=0, keepdims=True) for k in range(top)]
    items += [gates[k : k + 1, :] for k in range(top)]
    table = jnp.concatenate(
        [jnp.broadcast_to(item, (16, tokens)) for item in items]
        + [jnp.zeros((256 - 16 * len(items), tokens), F32)],
        axis=0,
    )
    place = iota(table.shape, 0) & 15
    meta = jnp.zeros((code.shape[0], 256), F32)
    for r in range(NODE_ROWS):
        meta += lax.dot_general(
            ones_where(code == float(r)).astype(BF),
            jnp.where(place == r, table, 0.0).astype(BF),
            (((1,), (1,)), ((), ())),
            preferred_element_type=F32,
        )
    return meta.astype(BF)


def pack_kernel(with_meta, piece_width, ids_ref, gates_ref, tok_ref, out_ref):
    ids = ids_ref[...]
    nodes = out_ref.shape[0] // NODE_BLOCK
    tokens = ids.shape[1]
    code = node_code(ids, nodes)
    inner = iota((NODE_BLOCK, tokens), 0)
    piece = steps(inner, NODE_ROWS, PIECES + 1)
    row = (inner - NODE_ROWS * piece).astype(F32)
    wanted = [jnp.where(piece == q, row, -9.0) for q in range(PIECES)]
    stacked = jnp.concatenate(
        [tok_ref[:, q * piece_width : (q + 1) * piece_width] for q in range(PIECES)], axis=0
    )
    if with_meta:
        meta = row_meta(ids, gates_ref[...].astype(F32), code)
        node_of, inner_of = steps(iota((GROUP_ROWS, nodes), 0), NODE_BLOCK, GROUP), None
        inner_of = iota((GROUP_ROWS, nodes), 0) - NODE_BLOCK * node_of
    for g in range(nodes // GROUP):
        picks = []
        for q in range(PIECES):
            picks.append(
                jnp.concatenate(
                    [ones_where(code[n : n + 1, :] == wanted[q]) for n in range(g * GROUP, (g + 1) * GROUP)],
                    axis=0,
                ).astype(BF)
            )
        rows = dot(jnp.concatenate(picks, axis=1), stacked)
        if with_meta:
            spot = (node_of + g * GROUP == iota((GROUP_ROWS, nodes), 1)) & (inner_of == PIECES * NODE_ROWS)
            rows += dot(ones_where(spot).astype(BF), meta)
        out_ref[g * GROUP_ROWS : (g + 1) * GROUP_ROWS, :] = rows.astype(BF)


def pack(ids_t, gates_t, tokens, nodes, chunk, with_meta):
    start, width = chunk
    span = PIECES * width
    return call(
        functools.partial(pack_kernel, with_meta, width),
        jax.ShapeDtypeStruct((nodes * NODE_BLOCK, width), BF),
        grid=(1,),
        in_specs=[
            pl.BlockSpec(ids_t.shape, lambda i: (0, 0)),
            pl.BlockSpec(gates_t.shape, lambda i: (0, 0)),
            pl.BlockSpec((tokens.shape[0], span), lambda i: (0, start // span)),
        ],
        out_specs=pl.BlockSpec((nodes * NODE_BLOCK, width), lambda i: (0, 0)),
        cost=5,
        name="pack_rows",
    )(ids_t, gates_t, tokens)


def expert_lanes(meta, expert, spread):
    ids = meta[:, :128]
    hit = ones_where(ids == (expert + 1).astype(F32))
    slot = dot((hit * (pltpu.roll(ids, 64, 1) + 1.0)).astype(BF), spread)
    gate = dot((hit * meta[:, 128:256]).astype(BF), spread)
    return slot, gate


def own_lane(values, node, g):
    part = values[g * GROUP : (g + 1) * GROUP, :]
    return jnp.sum(jnp.where(iota(part.shape, 0) == node, part, 0.0), axis=0, keepdims=True)


def lane_tables():
    node, piece, row = block_position((1, GROUP_ROWS), 1)
    lane = iota((128, GROUP_ROWS), 0)
    spread = ones_where(((lane & 15) == row) & (lane < 64)).astype(BF)
    return node, piece, spread


def row_target():
    row = iota((GROUP * SLOTS, GROUP_ROWS), 0)
    node = steps(row, SLOTS, GROUP)
    return (row + (8 - SLOTS) * node + 1).astype(F32)


def select_kernel(with_meta, where_ref, rows_ref, *out_refs):
    nodes = rows_ref.shape[0] // NODE_BLOCK
    width = rows_ref.shape[1]
    if with_meta:
        meta_ref, out_refs = out_refs[0], out_refs[1:]
        spot = iota((nodes, rows_ref.shape[0]), 1) == iota((nodes, rows_ref.shape[0]), 0) * NODE_BLOCK + PIECES * NODE_ROWS
        meta = dot(ones_where(spot).astype(BF), rows_ref[...])
        meta_ref[...] = meta
    else:
        meta, out_refs = out_refs[0][...], out_refs[1:]
    node, piece, spread = lane_tables()
    target = row_target()
    slots = []
    for d in range(EXPERTS):
        expert = where_ref[0] * EXPERTS + ((where_ref[1] + d) & (EXPERTS - 1))
        slots.append(expert_lanes(meta, expert, spread)[0])
    shift = 8.0 * node.astype(F32)
    held = [[None] * EXPERTS for _ in range(PIECES)]
    for g in range(nodes // GROUP):
        lines = [own_lane(slots[d], node, g) + shift for d in range(EXPERTS)]
        picks = []
        for q in range(PIECES):
            for d in range(EXPERTS):
                line = jnp.where(piece == q, lines[d], -9.0)
                picks.append(ones_where(target == line))
        picked = dot(
            jnp.concatenate(picks, axis=0).astype(BF), rows_ref[g * GROUP_ROWS : (g + 1) * GROUP_ROWS, :]
        )
        height = GROUP * SLOTS
        for q in range(PIECES):
            for d in range(EXPERTS):
                at = (q * EXPERTS + d) * height
                part = picked[at : at + height]
                if g % 2 == 0:
                    held[q][d] = part
                else:
                    both = jnp.concatenate([held[q][d], part], axis=0).astype(BF)
                    out_refs[d][(g - 1) * height : (g + 1) * height, q * width : (q + 1) * width] = both


def select(where, rows, meta, nodes):
    width = rows.shape[1]
    with_meta = meta is None
    shapes = [jax.ShapeDtypeStruct((nodes * SLOTS, PIECES * width), BF)] * EXPERTS
    if with_meta:
        shapes = [jax.ShapeDtypeStruct((nodes, 256), F32)] + shapes
    out = call(
        functools.partial(select_kernel, with_meta),
        shapes,
        in_specs=[
            pl.BlockSpec(memory_space=pltpu.SMEM),
        ]
        + [pl.BlockSpec(memory_space=pltpu.VMEM)] * (1 if with_meta else 2),
        cost=20,
        name="select_rows",
    )(where, rows, *(() if with_meta else (meta,)))
    return (out[0], out[1:]) if with_meta else (None, out)


def mix_kernel(where_ref, meta_ref, *refs):
    out_ref, value_refs = refs[-1], refs[:-1]
    nodes = out_ref.shape[0] // NODE_BLOCK
    width = out_ref.shape[1]
    meta = meta_ref[...]
    node, _, spread = lane_tables()
    target = row_target()
    tables = []
    for d in range(EXPERTS):
        expert = where_ref[0] * EXPERTS + ((where_ref[1] + d) & (EXPERTS - 1))
        tables.append(expert_lanes(meta, expert, spread))
    shift = 8.0 * node.astype(F32)
    _, out_piece, _ = block_position((GROUP_ROWS, width), 0)
    height = GROUP * SLOTS
    for g in range(nodes // GROUP):
        gated = []
        values = []
        for d in range(EXPERTS):
            line = own_lane(tables[d][0], node, g) + shift
            gate = own_lane(tables[d][1], node, g)
            gated.append(jnp.where(target == line, jnp.broadcast_to(gate, target.shape), 0.0))
            pair = value_refs[d][(g // 2) * 2 * height : (g // 2 + 1) * 2 * height, :].astype(F32)
            values.append(pair[(g % 2) * height : (g % 2 + 1) * height, :])
        share = lax.dot_general(
            jnp.concatenate(gated, axis=0).astype(BF),
            jnp.concatenate(values, axis=0).astype(BF),
            (((0,), (0,)), ((), ())),
            preferred_element_type=F32,
        )
        total = jnp.zeros((GROUP_ROWS, width), F32)
        for q in range(PIECES):
            total = jnp.where(out_piece == q, share[:, q * width : (q + 1) * width], total)
        out_ref[g * GROUP_ROWS : (g + 1) * GROUP_ROWS, :] = total.astype(BF)


def mix(where, meta, values, nodes):
    width = values[0].shape[1] // PIECES
    return call(
        mix_kernel,
        jax.ShapeDtypeStruct((nodes * NODE_BLOCK, width), BF),
        in_specs=[pl.BlockSpec(memory_space=pltpu.SMEM)]
        + [pl.BlockSpec(memory_space=pltpu.VMEM)] * (1 + len(values)),
        cost=40,
        name="node_share",
    )(where, meta, *values)


def finish_kernel(width, ids_ref, home_ref, *refs):
    out_ref = refs[-1]
    tokens, top = ids_ref.shape
    nodes = home_ref.shape[0] // NODE_BLOCK
    node = iota((tokens, nodes), 1)
    hit = jnp.zeros((tokens, nodes), F32)
    for k in range(top):
        hit = jnp.maximum(hit, ones_where((ids_ref[:, k : k + 1] >> 2) == node))
    before = ones_where(iota((tokens, tokens), 1) < iota((tokens, tokens), 0)).astype(BF)
    code = jnp.where(hit > 0, dot(before, hit.astype(BF)) + 1.0, 0.0).astype(BF)
    lane_node, piece, row = block_position((1, GROUP_ROWS), 1)
    total = jnp.zeros((PIECES * tokens, width), F32)
    for g in range(nodes // GROUP):
        spread = ones_where(iota((nodes, GROUP_ROWS), 0) == lane_node + g * GROUP).astype(BF)
        lanes = dot(code, spread)
        picks = []
        for q in range(PIECES):
            line = jnp.where(piece == q, row + 1, -9).astype(F32)
            picks.append(ones_where(lanes == line))
        total += dot(
            jnp.concatenate(picks, axis=0).astype(BF), home_ref[g * GROUP_ROWS : (g + 1) * GROUP_ROWS, :]
        )
    for q in range(PIECES):
        out_ref[:, q * width : (q + 1) * width] = total[q * tokens : (q + 1) * tokens, :].astype(BF)


def finish(ids, home, chunk, before, columns):
    start, width = chunk
    span = PIECES * width
    specs = [
        pl.BlockSpec(ids.shape, lambda i: (0, 0)),
        pl.BlockSpec(home.shape, lambda i: (0, 0)),
    ]
    args = [ids, home]
    aliases = {}
    if before is not None:
        specs.append(pl.BlockSpec(memory_space=pl.ANY))
        args.append(before)
        aliases = {2: 0}
    return call(
        functools.partial(finish_kernel, width),
        jax.ShapeDtypeStruct((ids.shape[0], columns), BF),
        grid=(1,),
        in_specs=specs,
        out_specs=pl.BlockSpec((ids.shape[0], span), lambda i: (0, start // span)),
        input_output_aliases=aliases,
        cost=6,
        name="sum_over_nodes",
    )(*args)


def up_kernel(start, down_start, *refs):
    last = down_start is not None
    count = 2 * EXPERTS
    blocks, (gate_ref, up_ref), refs = refs[:count], refs[count : count + 2], refs[count + 2 :]
    if last:
        sums_in, down_ref, refs = refs[:2], refs[2], refs[3:]
        (hidden_ref, other_out), (x_ref, wg_ref, wu_ref, *sums, wd_ref, other_ref, sems) = refs[:2], refs[2:]
    else:
        outs, (x_ref, wg_ref, wu_ref, sems) = refs[:2], refs[2:]
    rows, span = blocks[0].shape
    band = pl.ds(start, span)
    used = iter(range(64))

    def begin(source, target):
        copy = pltpu.make_async_copy(source, target, sems.at[next(used)])
        copy.start()
        return copy

    weights = [begin(gate_ref.at[0, band, :], wg_ref), begin(up_ref.at[0, band, :], wu_ref)]
    order = [EXPERTS, EXPERTS + 2, 0, 2] if last else [0, 2, EXPERTS, EXPERTS + 2]
    loads = {}
    for i in order:
        at = pl.ds(i * rows, 2 * rows)
        loads[i] = [begin(blocks[k], x_ref.at[pl.ds(k * rows, rows), :]) for k in (i, i + 1)]
        if last:
            loads[i] += [begin(source.at[at, :], target.at[at, :]) for source, target in zip(sums_in, sums)]
            if i == order[1]:
                weights_down = begin(down_ref.at[0, :, pl.ds(down_start, other_ref.shape[1])], wd_ref)
    for copy in weights:
        copy.wait()
    for i in order:
        for copy in loads[i]:
            copy.wait()
        at = pl.ds(i * rows, 2 * rows)
        gate = dot(x_ref[at, :], wg_ref[...])
        up = dot(x_ref[at, :], wu_ref[...])
        if last:
            gate += sums[0][at, :]
            up += sums[1][at, :]
            hidden_ref[at, :] = ((gate / (1.0 + jnp.exp(-gate))) * up).astype(BF)
            if i == order[1]:
                weights_down.wait()
                other_ref[...] = dot(hidden_ref[pl.ds(EXPERTS * rows, EXPERTS * rows), :], wd_ref[...]).astype(BF)
                sent = begin(other_ref, other_out)
        else:
            outs[0][at, :] = gate
            outs[1][at, :] = up
    if last:
        sent.wait()


def up_step(blocks, w_gate, w_up, chunk):
    start, width = chunk
    span = PIECES * width
    rows = blocks[0].shape[0] * len(blocks)
    units = w_gate.shape[2]
    any_spec = pl.BlockSpec(memory_space=pl.ANY)
    args = list(blocks) + [w_gate, w_up]
    return call(
        functools.partial(up_kernel, start, None),
        [jax.ShapeDtypeStruct((rows, units), F32)] * 2,
        in_specs=[any_spec] * len(args),
        scratch_shapes=[
            pltpu.VMEM((rows, span), BF),
            pltpu.VMEM((span, units), BF),
            pltpu.VMEM((span, units), BF),
            pltpu.SemaphoreType.DMA((2 + len(blocks),)),
        ],
        cost=40,
        name="gate_up",
    )(*args)


def hidden_step(blocks, w_gate, w_up, sums, w_down, chunk, down_chunk):
    start, width = chunk
    span, down_span = PIECES * width, PIECES * down_chunk[1]
    rows = blocks[0].shape[0] * len(blocks)
    units = w_gate.shape[2]
    any_spec = pl.BlockSpec(memory_space=pl.ANY)
    args = list(blocks) + [w_gate, w_up] + list(sums) + [w_down]
    return call(
        functools.partial(up_kernel, start, down_chunk[0]),
        [jax.ShapeDtypeStruct((rows, units), BF), jax.ShapeDtypeStruct((rows // 2, down_span), BF)],
        in_specs=[any_spec] * len(args),
        out_specs=[pl.BlockSpec(memory_space=pltpu.VMEM), any_spec],
        scratch_shapes=[
            pltpu.VMEM((rows, span), BF),
            pltpu.VMEM((span, units), BF),
            pltpu.VMEM((span, units), BF),
            pltpu.VMEM((rows, units), F32),
            pltpu.VMEM((rows, units), F32),
            pltpu.VMEM((units, down_span), BF),
            pltpu.VMEM((rows // 2, down_span), BF),
            pltpu.SemaphoreType.DMA((4 + 3 * len(blocks),)),
        ],
        cost=10,
        name="hidden_down",
    )(*args)


def down_other_kernel(hidden_ref, w_ref, out_ref):
    out_ref[...] = dot(hidden_ref[...], w_ref[0]).astype(BF)


def down_own_kernel(hidden_ref, w_ref, mate_ref, *out_refs):
    mine = dot(hidden_ref[...], w_ref[0]).astype(BF)
    value = (mine.astype(F32) + mate_ref[...].astype(F32)).astype(BF)
    rows = out_refs[0].shape[0]
    for d, out_ref in enumerate(out_refs):
        out_ref[...] = value[d * rows : (d + 1) * rows, :]


def down_other(hidden, w_down, chunk):
    start, width = chunk
    span = PIECES * width
    tile = 896
    rows, units = hidden.shape[0] // 2, hidden.shape[1]
    return call(
        down_other_kernel,
        jax.ShapeDtypeStruct((rows, span), BF),
        grid=(span // tile,),
        in_specs=[
            pl.BlockSpec((rows, units), lambda i: (1, 0)),
            pl.BlockSpec((1, units, tile), lambda i: (0, 0, start // tile + i)),
        ],
        out_specs=pl.BlockSpec((rows, tile), lambda i: (0, i)),
        cost=4,
        name="down_other",
    )(hidden, w_down)


def down_own(hidden, w_down, mate, chunk):
    start, width = chunk
    span = PIECES * width
    tile = 896
    rows, units = hidden.shape[0] // 2, hidden.shape[1]
    part = rows // EXPERTS
    return call(
        down_own_kernel,
        [jax.ShapeDtypeStruct((part, span), BF)] * EXPERTS,
        grid=(span // tile,),
        in_specs=[
            pl.BlockSpec((rows, units), lambda i: (0, 0)),
            pl.BlockSpec((1, units, tile), lambda i: (0, 0, start // tile + i)),
            pl.BlockSpec((rows, tile), lambda i: (0, i)),
        ],
        out_specs=[pl.BlockSpec((part, tile), lambda i: (0, i))] * EXPERTS,
        cost=4,
        name="down_own",
    )(hidden, w_down, mate)


def over_nodes(rows, nodes):
    cut = rows.reshape(nodes, NODE_BLOCK, rows.shape[1])
    return lax.all_to_all(cut, "node", split_axis=0, concat_axis=0, tiled=True).reshape(rows.shape)


def along_y(block, distance):
    pairs = [(y * 2 + c, ((y + distance) % EXPERTS) * 2 + c) for y in range(EXPERTS) for c in range(2)]
    return lax.ppermute(block, "local", pairs)


def to_mate(block):
    return lax.ppermute(block, "local", [(i, i ^ 1) for i in range(2 * EXPERTS)])


def per_device(tokens, expert_ids, gate_weights, w_gate, w_up, w_down):
    nodes = lax.axis_size("node")
    columns = tokens.shape[1]
    where = jnp.stack([lax.axis_index("node"), lax.axis_index("local") // 2]).astype(jnp.int32)
    ids_t = expert_ids.T
    gates_t = gate_weights.T
    first, second = CHUNKS
    packed = [pack(ids_t, gates_t, tokens, nodes, chunk, chunk is first) for chunk in CHUNKS]
    packed[1], where = lax.optimization_barrier((packed[1], where))
    arrived = [over_nodes(rows, nodes) for rows in packed]
    meta, blocks = select(where, arrived[0], None, nodes)
    own = [blocks[0]] + [along_y(blocks[d], d) for d in range(1, EXPERTS)]
    near = to_mate(blocks[0])
    _, blocks = select(where, arrived[1], meta, nodes)
    own, near, blocks = lax.optimization_barrier((own, near, blocks))
    later = [along_y(blocks[d], d) for d in range(1, EXPERTS)]
    later_near = to_mate(blocks[0])
    sums = up_step(own + [near] + [to_mate(block) for block in own[1:]], w_gate, w_up, first)
    later, sums = lax.optimization_barrier((later, sums))
    own = [blocks[0]] + later
    hidden, other = hidden_step(
        own + [later_near] + [to_mate(block) for block in later], w_gate, w_up, sums, w_down, second, first
    )
    mate = to_mate(other)
    later_mate = to_mate(down_other(hidden, w_down, second))
    values = down_own(hidden, w_down, mate, first)
    back = [values[0]] + [along_y(values[d], -d) for d in range(1, EXPERTS)]
    values = down_own(hidden, w_down, later_mate, second)
    back, values = lax.optimization_barrier((back, values))
    later_back = [values[0]] + [along_y(values[d], -d) for d in range(1, EXPERTS)]
    mixed = None
    for chunk, rows in ((first, back), (second, later_back)):
        home = over_nodes(mix(where, meta, rows, nodes), nodes)
        mixed = finish(expert_ids, home, chunk, mixed, columns)
    return mixed


def solution(mesh):
    rows = P(("node", "local"), None)
    cube = P(("node", "local"), None, None)
    return jax.shard_map(
        per_device,
        mesh=mesh,
        in_specs=(rows, rows, rows, cube, cube, cube),
        out_specs=rows,
        check_vma=False,
    )
```

```python
import functools
from typing import NamedTuple

import jax
import jax.numpy as jnp
from jax import lax
from jax.experimental import pallas as pl
from jax.experimental.pallas import tpu as pltpu
from jax.sharding import PartitionSpec as P

SLOTS = 5
EXPERTS = 4
NODE_ROWS = EXPERTS * SLOTS // 2
GROUP = 8


class Chunk(NamedTuple):
    start: int
    width: int
    pieces: int
    block: int

    @property
    def span(self):
        return self.width * self.pieces

    @property
    def group(self):
        return self.block * GROUP


OUT = (Chunk(0, 512, 3, 32), Chunk(1536, 512, 4, 40))
HOME = (Chunk(0, 384, 4, 40), Chunk(1536, 512, 4, 40))
BF = jnp.bfloat16
F32 = jnp.float32
VMEM = 63 << 20


def dot(a, b):
    return jnp.dot(a, b, preferred_element_type=F32)


def iota(shape, dim):
    return lax.broadcasted_iota(jnp.int32, shape, dim)


def steps(value, step, count):
    total = jnp.zeros_like(value)
    for i in range(1, count):
        total = total + jnp.where(value >= step * i, 1, 0)
    return total


def ones_where(mask):
    return jnp.where(mask, 1.0, 0.0).astype(F32)


def block_position(shape, dim, chunk):
    index = iota(shape, dim)
    node = steps(index, chunk.block, GROUP)
    inner = index - chunk.block * node
    piece = steps(inner, NODE_ROWS, chunk.pieces + 1)
    return node, piece, inner - NODE_ROWS * piece


def call(kernel, out_shape, cost, **kwargs):
    return pl.pallas_call(
        kernel,
        out_shape=out_shape,
        cost_estimate=pl.CostEstimate(flops=cost * 10**9, bytes_accessed=10**6, transcendentals=0),
        compiler_params=pltpu.CompilerParams(vmem_limit_bytes=VMEM),
        **kwargs,
    )


def node_code(ids, nodes):
    node = iota((nodes, ids.shape[1]), 0)
    hit = jnp.zeros(node.shape, F32)
    for k in range(ids.shape[0]):
        hit = jnp.maximum(hit, ones_where((ids[k : k + 1, :] >> 2) == node))
    tokens = ids.shape[1]
    before = ones_where(iota((tokens, tokens), 0) < iota((tokens, tokens), 1)).astype(BF)
    return jnp.where(hit > 0, dot(hit.astype(BF), before), -1.0)


def row_meta(ids, gates, code):
    top, tokens = ids.shape
    expert = iota((128, tokens), 0)
    hits = [ones_where(ids[k : k + 1, :] == expert) for k in range(top)]
    before = ones_where(iota((tokens, tokens), 0) < iota((tokens, tokens), 1)).astype(BF)
    rank = dot(functools.reduce(jnp.maximum, hits).astype(BF), before)
    items = [(ids[k : k + 1, :] + 1).astype(F32) for k in range(top)]
    items += [jnp.sum(hits[k] * rank, axis=0, keepdims=True) for k in range(top)]
    items += [gates[k : k + 1, :] for k in range(top)]
    table = jnp.concatenate(
        [jnp.broadcast_to(item, (16, tokens)) for item in items]
        + [jnp.zeros((256 - 16 * len(items), tokens), F32)],
        axis=0,
    )
    place = iota(table.shape, 0) & 15
    meta = jnp.zeros((code.shape[0], 256), F32)
    for r in range(NODE_ROWS):
        meta += lax.dot_general(
            ones_where(code == float(r)).astype(BF),
            jnp.where(place == r, table, 0.0).astype(BF),
            (((1,), (1,)), ((), ())),
            preferred_element_type=F32,
        )
    return meta.astype(BF)


def pack_kernel(chunk, with_meta, ids_ref, gates_ref, tok_ref, out_ref):
    ids = ids_ref[...]
    nodes = out_ref.shape[0] // chunk.block
    tokens = ids.shape[1]
    code = node_code(ids, nodes)
    inner = iota((chunk.block, tokens), 0)
    piece = steps(inner, NODE_ROWS, chunk.pieces + 1)
    row = (inner - NODE_ROWS * piece).astype(F32)
    wanted = [jnp.where(piece == q, row, -9.0) for q in range(chunk.pieces)]
    first = [chunk.start + q * chunk.width for q in range(chunk.pieces)]
    stacked = jnp.concatenate([tok_ref[:, at : at + chunk.width] for at in first], axis=0)
    if with_meta:
        meta = row_meta(ids, gates_ref[...].astype(F32), code)
        meta = jnp.concatenate([meta, jnp.zeros((nodes, chunk.width - 256), BF)], axis=1)
        node_of = steps(iota((chunk.group, nodes), 0), chunk.block, GROUP)
        inner_of = iota((chunk.group, nodes), 0) - chunk.block * node_of
    for g in range(nodes // GROUP):
        picks = []
        for q in range(chunk.pieces):
            picks.append(
                jnp.concatenate(
                    [ones_where(code[n : n + 1, :] == wanted[q]) for n in range(g * GROUP, (g + 1) * GROUP)],
                    axis=0,
                ).astype(BF)
            )
        rows = dot(jnp.concatenate(picks, axis=1), stacked)
        if with_meta:
            spot = (node_of + g * GROUP == iota((chunk.group, nodes), 1)) & (inner_of == chunk.pieces * NODE_ROWS)
            rows += dot(ones_where(spot).astype(BF), meta)
        out_ref[g * chunk.group : (g + 1) * chunk.group, :] = rows.astype(BF)


def pack(ids_t, gates_t, tokens, nodes, chunk, with_meta):
    return call(
        functools.partial(pack_kernel, chunk, with_meta),
        jax.ShapeDtypeStruct((nodes * chunk.block, chunk.width), BF),
        cost=5,
        name="pack_rows",
    )(ids_t, gates_t, tokens)


def expert_lanes(meta, expert, spread):
    ids = meta[:, :128]
    hit = ones_where(ids == (expert + 1).astype(F32))
    slot = dot((hit * (pltpu.roll(ids, 64, 1) + 1.0)).astype(BF), spread)
    gate = dot((hit * meta[:, 128:256]).astype(BF), spread)
    return slot, gate


def own_lane(values, node, g):
    part = values[g * GROUP : (g + 1) * GROUP, :]
    return jnp.sum(jnp.where(iota(part.shape, 0) == node, part, 0.0), axis=0, keepdims=True)


def lane_tables(chunk):
    node, piece, row = block_position((1, chunk.group), 1, chunk)
    lane = iota((128, chunk.group), 0)
    spread = ones_where(((lane & 15) == row) & (lane < 64)).astype(BF)
    return node, piece, spread


def row_target(chunk):
    row = iota((GROUP * SLOTS, chunk.group), 0)
    node = steps(row, SLOTS, GROUP)
    return (row + (8 - SLOTS) * node + 1).astype(F32)


def select_kernel(chunk, with_meta, where_ref, rows_ref, *out_refs):
    nodes = rows_ref.shape[0] // chunk.block
    width = chunk.width
    if with_meta:
        meta_ref, out_refs = out_refs[0], out_refs[1:]
        shape = (nodes, rows_ref.shape[0])
        spot = iota(shape, 1) == iota(shape, 0) * chunk.block + chunk.pieces * NODE_ROWS
        meta = dot(ones_where(spot).astype(BF), rows_ref[:, :256])
        meta_ref[...] = meta
    else:
        meta, out_refs = out_refs[0][...], out_refs[1:]
    node, piece, spread = lane_tables(chunk)
    target = row_target(chunk)
    slots = []
    for d in range(EXPERTS):
        expert = where_ref[0] * EXPERTS + ((where_ref[1] + d) & (EXPERTS - 1))
        slots.append(expert_lanes(meta, expert, spread)[0])
    shift = 8.0 * node.astype(F32)
    held = [[None] * EXPERTS for _ in range(chunk.pieces)]
    for g in range(nodes // GROUP):
        lines = [own_lane(slots[d], node, g) + shift for d in range(EXPERTS)]
        picks = []
        for q in range(chunk.pieces):
            for d in range(EXPERTS):
                line = jnp.where(piece == q, lines[d], -9.0)
                picks.append(ones_where(target == line))
        picked = dot(
            jnp.concatenate(picks, axis=0).astype(BF), rows_ref[g * chunk.group : (g + 1) * chunk.group, :]
        )
        height = GROUP * SLOTS
        for q in range(chunk.pieces):
            for d in range(EXPERTS):
                at = (q * EXPERTS + d) * height
                part = picked[at : at + height]
                if g % 2 == 0:
                    held[q][d] = part
                else:
                    both = jnp.concatenate([held[q][d], part], axis=0).astype(BF)
                    out_refs[d][(g - 1) * height : (g + 1) * height, q * width : (q + 1) * width] = both


def select(where, rows, meta, nodes, chunk):
    with_meta = meta is None
    shapes = [jax.ShapeDtypeStruct((nodes * SLOTS, chunk.span), BF)] * EXPERTS
    if with_meta:
        shapes = [jax.ShapeDtypeStruct((nodes, 256), F32)] + shapes
    out = call(
        functools.partial(select_kernel, chunk, with_meta),
        shapes,
        in_specs=[
            pl.BlockSpec(memory_space=pltpu.SMEM),
        ]
        + [pl.BlockSpec(memory_space=pltpu.VMEM)] * (1 if with_meta else 2),
        cost=20,
        name="select_rows",
    )(where, rows, *(() if with_meta else (meta,)))
    return (out[0], out[1:]) if with_meta else (None, out)


def mix_kernel(chunk, where_ref, meta_ref, *refs):
    out_ref, value_refs = refs[-1], refs[:-1]
    nodes = out_ref.shape[0] // chunk.block
    width = chunk.width
    meta = meta_ref[...]
    node, _, spread = lane_tables(chunk)
    target = row_target(chunk)
    tables = []
    for d in range(EXPERTS):
        expert = where_ref[0] * EXPERTS + ((where_ref[1] + d) & (EXPERTS - 1))
        tables.append(expert_lanes(meta, expert, spread))
    shift = 8.0 * node.astype(F32)
    _, out_piece, _ = block_position((chunk.group, width), 0, chunk)
    height = GROUP * SLOTS
    for g in range(nodes // GROUP):
        gated = []
        values = []
        for d in range(EXPERTS):
            line = own_lane(tables[d][0], node, g) + shift
            gate = own_lane(tables[d][1], node, g)
            gated.append(jnp.where(target == line, jnp.broadcast_to(gate, target.shape), 0.0))
            pair = value_refs[d][(g // 2) * 2 * height : (g // 2 + 1) * 2 * height, :].astype(F32)
            values.append(pair[(g % 2) * height : (g % 2 + 1) * height, :])
        share = lax.dot_general(
            jnp.concatenate(gated, axis=0).astype(BF),
            jnp.concatenate(values, axis=0).astype(BF),
            (((0,), (0,)), ((), ())),
            preferred_element_type=F32,
        )
        total = jnp.zeros((chunk.group, width), F32)
        for q in range(chunk.pieces):
            total = jnp.where(out_piece == q, share[:, q * width : (q + 1) * width], total)
        out_ref[g * chunk.group : (g + 1) * chunk.group, :] = total.astype(BF)


def mix(where, meta, values, nodes, chunk):
    return call(
        functools.partial(mix_kernel, chunk),
        jax.ShapeDtypeStruct((nodes * chunk.block, chunk.width), BF),
        in_specs=[pl.BlockSpec(memory_space=pltpu.SMEM)]
        + [pl.BlockSpec(memory_space=pltpu.VMEM)] * (1 + len(values)),
        cost=40,
        name="node_share",
    )(where, meta, *values)


def finish_kernel(chunk, ids_ref, home_ref, *refs):
    out_ref = refs[-1]
    at = 0
    if len(refs) > 1:
        at = chunk.start
        out_ref[:, :at] = refs[0][...]
    tokens, top = ids_ref.shape
    nodes = home_ref.shape[0] // chunk.block
    node = iota((tokens, nodes), 1)
    hit = jnp.zeros((tokens, nodes), F32)
    for k in range(top):
        hit = jnp.maximum(hit, ones_where((ids_ref[:, k : k + 1] >> 2) == node))
    before = ones_where(iota((tokens, tokens), 1) < iota((tokens, tokens), 0)).astype(BF)
    code = jnp.where(hit > 0, dot(before, hit.astype(BF)) + 1.0, 0.0).astype(BF)
    lane_node, piece, row = block_position((1, chunk.group), 1, chunk)
    total = jnp.zeros((chunk.pieces * tokens, chunk.width), F32)
    for g in range(nodes // GROUP):
        spread = ones_where(iota((nodes, chunk.group), 0) == lane_node + g * GROUP).astype(BF)
        lanes = dot(code, spread)
        picks = []
        for q in range(chunk.pieces):
            line = jnp.where(piece == q, row + 1, -9).astype(F32)
            picks.append(ones_where(lanes == line))
        total += dot(
            jnp.concatenate(picks, axis=0).astype(BF), home_ref[g * chunk.group : (g + 1) * chunk.group, :]
        )
    for q in range(chunk.pieces):
        column = at + q * chunk.width
        out_ref[:, column : column + chunk.width] = total[q * tokens : (q + 1) * tokens, :].astype(BF)


def finish(ids, home, chunk, *before):
    columns = chunk.span + (chunk.start if before else 0)
    return call(
        functools.partial(finish_kernel, chunk),
        jax.ShapeDtypeStruct((ids.shape[0], columns), BF),
        cost=6,
        name="sum_over_nodes",
    )(ids, home, *before)


def up_kernel(start, down_start, *refs):
    last = down_start is not None
    count = 2 * EXPERTS
    blocks, (gate_ref, up_ref), refs = refs[:count], refs[count : count + 2], refs[count + 2 :]
    if last:
        sums_in, down_ref, refs = refs[:2], refs[2], refs[3:]
        (hidden_ref, other_out), (x_ref, wg_ref, wu_ref, *sums, wd_ref, other_ref, sems) = refs[:2], refs[2:]
    else:
        outs, (x_ref, wg_ref, wu_ref, sems) = refs[:2], refs[2:]
    rows, span = blocks[0].shape
    band = pl.ds(start, span)
    used = iter(range(64))

    def begin(source, target):
        copy = pltpu.make_async_copy(source, target, sems.at[next(used)])
        copy.start()
        return copy

    weights = [begin(gate_ref.at[0, band, :], wg_ref), begin(up_ref.at[0, band, :], wu_ref)]
    order = [EXPERTS, EXPERTS + 2, 0, 2] if last else [0, 2, EXPERTS, EXPERTS + 2]
    loads = {}
    for i in order:
        at = pl.ds(i * rows, 2 * rows)
        loads[i] = [begin(blocks[k], x_ref.at[pl.ds(k * rows, rows), :]) for k in (i, i + 1)]
        if last:
            loads[i] += [begin(source.at[at, :], target.at[at, :]) for source, target in zip(sums_in, sums)]
            if i == order[1]:
                weights_down = begin(down_ref.at[0, :, pl.ds(down_start, other_ref.shape[1])], wd_ref)
    for copy in weights:
        copy.wait()
    for i in order:
        for copy in loads[i]:
            copy.wait()
        at = pl.ds(i * rows, 2 * rows)
        gate = dot(x_ref[at, :], wg_ref[...])
        up = dot(x_ref[at, :], wu_ref[...])
        if last:
            gate += sums[0][at, :]
            up += sums[1][at, :]
            hidden_ref[at, :] = ((gate / (1.0 + jnp.exp(-gate))) * up).astype(BF)
            if i == order[1]:
                weights_down.wait()
                other_ref[...] = dot(hidden_ref[pl.ds(EXPERTS * rows, EXPERTS * rows), :], wd_ref[...]).astype(BF)
                sent = begin(other_ref, other_out)
        else:
            outs[0][at, :] = gate
            outs[1][at, :] = up
    if last:
        sent.wait()


def up_step(blocks, w_gate, w_up, chunk):
    span = chunk.span
    rows = blocks[0].shape[0] * len(blocks)
    units = w_gate.shape[2]
    any_spec = pl.BlockSpec(memory_space=pl.ANY)
    args = list(blocks) + [w_gate, w_up]
    return call(
        functools.partial(up_kernel, chunk.start, None),
        [jax.ShapeDtypeStruct((rows, units), F32)] * 2,
        in_specs=[any_spec] * len(args),
        scratch_shapes=[
            pltpu.VMEM((rows, span), BF),
            pltpu.VMEM((span, units), BF),
            pltpu.VMEM((span, units), BF),
            pltpu.SemaphoreType.DMA((2 + len(blocks),)),
        ],
        cost=40,
        name="gate_up",
    )(*args)


def hidden_step(blocks, w_gate, w_up, sums, w_down, chunk, down_chunk):
    span, down_span = chunk.span, down_chunk.span
    rows = blocks[0].shape[0] * len(blocks)
    units = w_gate.shape[2]
    any_spec = pl.BlockSpec(memory_space=pl.ANY)
    args = list(blocks) + [w_gate, w_up] + list(sums) + [w_down]
    return call(
        functools.partial(up_kernel, chunk.start, down_chunk.start),
        [jax.ShapeDtypeStruct((rows, units), BF), jax.ShapeDtypeStruct((rows // 2, down_span), BF)],
        in_specs=[any_spec] * len(args),
        out_specs=[pl.BlockSpec(memory_space=pltpu.VMEM), any_spec],
        scratch_shapes=[
            pltpu.VMEM((rows, span), BF),
            pltpu.VMEM((span, units), BF),
            pltpu.VMEM((span, units), BF),
            pltpu.VMEM((rows, units), F32),
            pltpu.VMEM((rows, units), F32),
            pltpu.VMEM((units, down_span), BF),
            pltpu.VMEM((rows // 2, down_span), BF),
            pltpu.SemaphoreType.DMA((4 + 3 * len(blocks),)),
        ],
        cost=10,
        name="hidden_down",
    )(*args)


def down_other_kernel(hidden_ref, w_ref, out_ref):
    out_ref[...] = dot(hidden_ref[...], w_ref[0]).astype(BF)


def down_own_kernel(hidden_ref, w_ref, mate_ref, *out_refs):
    mine = dot(hidden_ref[...], w_ref[0]).astype(BF)
    value = (mine.astype(F32) + mate_ref[...].astype(F32)).astype(BF)
    rows = out_refs[0].shape[0]
    for d, out_ref in enumerate(out_refs):
        out_ref[...] = value[d * rows : (d + 1) * rows, :]


def down_other(hidden, w_down, chunk):
    start, span = chunk.start, chunk.span
    tile = 768 if start == 0 else 512
    rows, units = hidden.shape[0] // 2, hidden.shape[1]
    return call(
        down_other_kernel,
        jax.ShapeDtypeStruct((rows, span), BF),
        grid=(span // tile,),
        in_specs=[
            pl.BlockSpec((rows, units), lambda i: (1, 0)),
            pl.BlockSpec((1, units, tile), lambda i: (0, 0, start // tile + i)),
        ],
        out_specs=pl.BlockSpec((rows, tile), lambda i: (0, i)),
        cost=4,
        name="down_other",
    )(hidden, w_down)


def down_own(hidden, w_down, mate, chunk):
    start, span = chunk.start, chunk.span
    tile = 768 if start == 0 else 512
    rows, units = hidden.shape[0] // 2, hidden.shape[1]
    part = rows // EXPERTS
    return call(
        down_own_kernel,
        [jax.ShapeDtypeStruct((part, span), BF)] * EXPERTS,
        grid=(span // tile,),
        in_specs=[
            pl.BlockSpec((rows, units), lambda i: (0, 0)),
            pl.BlockSpec((1, units, tile), lambda i: (0, 0, start // tile + i)),
            pl.BlockSpec((rows, tile), lambda i: (0, i)),
        ],
        out_specs=[pl.BlockSpec((part, tile), lambda i: (0, i))] * EXPERTS,
        cost=10 if chunk.start == 0 else 4,
        name="down_own",
    )(hidden, w_down, mate)


def over_nodes(rows, nodes):
    cut = rows.reshape(nodes, rows.shape[0] // nodes, rows.shape[1])
    return lax.all_to_all(cut, "node", split_axis=0, concat_axis=0, tiled=True).reshape(rows.shape)


def along_y(block, distance):
    pairs = [(y * 2 + c, ((y + distance) % EXPERTS) * 2 + c) for y in range(EXPERTS) for c in range(2)]
    return lax.ppermute(block, "local", pairs)


def to_mate(block):
    return lax.ppermute(block, "local", [(i, i ^ 1) for i in range(2 * EXPERTS)])


def per_device(tokens, expert_ids, gate_weights, w_gate, w_up, w_down):
    nodes = lax.axis_size("node")
    where = jnp.stack([lax.axis_index("node"), lax.axis_index("local") // 2]).astype(jnp.int32)
    ids_t = expert_ids.T
    gates_t = gate_weights.T
    packed = [pack(ids_t, gates_t, tokens, nodes, chunk, chunk is OUT[0]) for chunk in OUT]
    packed[1], where = lax.optimization_barrier((packed[1], where))
    arrived = [over_nodes(rows, nodes) for rows in packed]
    meta, blocks = select(where, arrived[0], None, nodes, OUT[0])
    own = [blocks[0]] + [along_y(blocks[d], d) for d in range(1, EXPERTS)]
    near = to_mate(blocks[0])
    _, blocks = select(where, arrived[1], meta, nodes, OUT[1])
    own, near, blocks = lax.optimization_barrier((own, near, blocks))
    later = [along_y(blocks[d], d) for d in range(1, EXPERTS)]
    later_near = to_mate(blocks[0])
    sums = up_step(own + [near] + [to_mate(block) for block in own[1:]], w_gate, w_up, OUT[0])
    later, sums = lax.optimization_barrier((later, sums))
    own = [blocks[0]] + later
    hidden, other = hidden_step(
        own + [later_near] + [to_mate(block) for block in later], w_gate, w_up, sums, w_down, OUT[1], HOME[0]
    )
    mate = to_mate(other)
    later_mate = to_mate(down_other(hidden, w_down, HOME[1]))
    values = down_own(hidden, w_down, mate, HOME[0])
    back = [values[0]] + [along_y(values[d], -d) for d in range(1, EXPERTS)]
    values = down_own(hidden, w_down, later_mate, HOME[1])
    back, values = lax.optimization_barrier((back, values))
    later_back = [values[0]] + [along_y(values[d], -d) for d in range(1, EXPERTS)]
    home = over_nodes(mix(where, meta, back, nodes, HOME[0]), nodes)
    later_home = over_nodes(mix(where, meta, later_back, nodes, HOME[1]), nodes)
    return finish(expert_ids, later_home, HOME[1], finish(expert_ids, home, HOME[0]))


def solution(mesh):
    rows = P(("node", "local"), None)
    cube = P(("node", "local"), None, None)
    return jax.shard_map(
        per_device,
        mesh=mesh,
        in_specs=(rows, rows, rows, cube, cube, cube),
        out_specs=rows,
        check_vma=False,
    )
```

```python
import functools
from typing import NamedTuple

import jax
import jax.numpy as jnp
from jax import lax
from jax.experimental import pallas as pl
from jax.experimental.pallas import tpu as pltpu
from jax.sharding import PartitionSpec as P

SLOTS = 5
EXPERTS = 4
NODE_ROWS = EXPERTS * SLOTS // 2
GROUP = 8


class Chunk(NamedTuple):
    start: int
    width: int
    pieces: int
    block: int

    @property
    def span(self):
        return self.width * self.pieces

    @property
    def group(self):
        return self.block * GROUP


OUT = (Chunk(0, 512, 3, 32), Chunk(1536, 512, 4, 40))
HOME = (Chunk(0, 384, 4, 40), Chunk(1536, 512, 4, 40))
BF = jnp.bfloat16
F32 = jnp.float32
VMEM = 63 << 20


def dot(a, b):
    return jnp.dot(a, b, preferred_element_type=F32)


def iota(shape, dim):
    return lax.broadcasted_iota(jnp.int32, shape, dim)


def steps(value, step, count):
    total = jnp.zeros_like(value)
    for i in range(1, count):
        total = total + jnp.where(value >= step * i, 1, 0)
    return total


def ones_where(mask):
    return jnp.where(mask, 1.0, 0.0).astype(F32)


def block_position(shape, dim, chunk):
    index = iota(shape, dim)
    node = steps(index, chunk.block, GROUP)
    inner = index - chunk.block * node
    piece = steps(inner, NODE_ROWS, chunk.pieces + 1)
    return node, piece, inner - NODE_ROWS * piece


def call(kernel, out_shape, cost, **kwargs):
    return pl.pallas_call(
        kernel,
        out_shape=out_shape,
        cost_estimate=pl.CostEstimate(flops=cost * 10**9, bytes_accessed=10**6, transcendentals=0),
        compiler_params=pltpu.CompilerParams(vmem_limit_bytes=VMEM),
        **kwargs,
    )


def node_code(ids, nodes):
    node = iota((nodes, ids.shape[1]), 0)
    hit = jnp.zeros(node.shape, F32)
    for k in range(ids.shape[0]):
        hit = jnp.maximum(hit, ones_where((ids[k : k + 1, :] >> 2) == node))
    tokens = ids.shape[1]
    before = ones_where(iota((tokens, tokens), 0) < iota((tokens, tokens), 1)).astype(BF)
    return jnp.where(hit > 0, dot(hit.astype(BF), before), -1.0)


def row_meta(ids, gates, code):
    top, tokens = ids.shape
    expert = iota((128, tokens), 0)
    hits = [ones_where(ids[k : k + 1, :] == expert) for k in range(top)]
    before = ones_where(iota((tokens, tokens), 0) < iota((tokens, tokens), 1)).astype(BF)
    rank = dot(functools.reduce(jnp.maximum, hits).astype(BF), before)
    items = [(ids[k : k + 1, :] + 1).astype(F32) for k in range(top)]
    items += [jnp.sum(hits[k] * rank, axis=0, keepdims=True) for k in range(top)]
    items += [gates[k : k + 1, :] for k in range(top)]
    table = jnp.concatenate(
        [jnp.broadcast_to(item, (16, tokens)) for item in items]
        + [jnp.zeros((256 - 16 * len(items), tokens), F32)],
        axis=0,
    )
    place = iota(table.shape, 0) & 15
    meta = jnp.zeros((code.shape[0], 256), F32)
    for r in range(NODE_ROWS):
        meta += lax.dot_general(
            ones_where(code == float(r)).astype(BF),
            jnp.where(place == r, table, 0.0).astype(BF),
            (((1,), (1,)), ((), ())),
            preferred_element_type=F32,
        )
    return meta.astype(BF)


def pack_kernel(chunk, with_meta, ids_ref, gates_ref, tok_ref, out_ref):
    ids = ids_ref[...]
    nodes = out_ref.shape[0] // chunk.block
    tokens = ids.shape[1]
    code = node_code(ids, nodes)
    inner = iota((chunk.block, tokens), 0)
    piece = steps(inner, NODE_ROWS, chunk.pieces + 1)
    row = (inner - NODE_ROWS * piece).astype(F32)
    wanted = [jnp.where(piece == q, row, -9.0) for q in range(chunk.pieces)]
    first = [chunk.start + q * chunk.width for q in range(chunk.pieces)]
    stacked = jnp.concatenate([tok_ref[:, at : at + chunk.width] for at in first], axis=0)
    if with_meta:
        meta = row_meta(ids, gates_ref[...].astype(F32), code)
        meta = jnp.concatenate([meta, jnp.zeros((nodes, chunk.width - 256), BF)], axis=1)
        node_of = steps(iota((chunk.group, nodes), 0), chunk.block, GROUP)
        inner_of = iota((chunk.group, nodes), 0) - chunk.block * node_of
    for g in range(nodes // GROUP):
        picks = []
        for q in range(chunk.pieces):
            picks.append(
                jnp.concatenate(
                    [ones_where(code[n : n + 1, :] == wanted[q]) for n in range(g * GROUP, (g + 1) * GROUP)],
                    axis=0,
                ).astype(BF)
            )
        rows = dot(jnp.concatenate(picks, axis=1), stacked)
        if with_meta:
            spot = (node_of + g * GROUP == iota((chunk.group, nodes), 1)) & (inner_of == chunk.pieces * NODE_ROWS)
            rows += dot(ones_where(spot).astype(BF), meta)
        out_ref[g * chunk.group : (g + 1) * chunk.group, :] = rows.astype(BF)


def pack(ids_t, gates_t, tokens, nodes, chunk, with_meta):
    return call(
        functools.partial(pack_kernel, chunk, with_meta),
        jax.ShapeDtypeStruct((nodes * chunk.block, chunk.width), BF),
        cost=5,
        name="pack_rows",
    )(ids_t, gates_t, tokens)


def expert_lanes(meta, expert, spread):
    ids = meta[:, :128]
    hit = ones_where(ids == (expert + 1).astype(F32))
    slot = dot((hit * (pltpu.roll(ids, 64, 1) + 1.0)).astype(BF), spread)
    gate = dot((hit * meta[:, 128:256]).astype(BF), spread)
    return slot, gate


def own_lane(values, node, g):
    part = values[g * GROUP : (g + 1) * GROUP, :]
    return jnp.sum(jnp.where(iota(part.shape, 0) == node, part, 0.0), axis=0, keepdims=True)


def lane_tables(chunk):
    node, piece, row = block_position((1, chunk.group), 1, chunk)
    lane = iota((128, chunk.group), 0)
    spread = ones_where(((lane & 15) == row) & (lane < 64)).astype(BF)
    return node, piece, spread


def row_target(chunk):
    row = iota((GROUP * SLOTS, chunk.group), 0)
    node = steps(row, SLOTS, GROUP)
    return (row + (8 - SLOTS) * node + 1).astype(F32)


def select_kernel(chunk, with_meta, where_ref, rows_ref, *out_refs):
    nodes = rows_ref.shape[0] // chunk.block
    width = chunk.width
    if with_meta:
        meta_ref, out_refs = out_refs[0], out_refs[1:]
        shape = (nodes, rows_ref.shape[0])
        spot = iota(shape, 1) == iota(shape, 0) * chunk.block + chunk.pieces * NODE_ROWS
        meta = dot(ones_where(spot).astype(BF), rows_ref[:, :256])
        meta_ref[...] = meta
    else:
        meta, out_refs = out_refs[0][...], out_refs[1:]
    node, piece, spread = lane_tables(chunk)
    target = row_target(chunk)
    slots = []
    for d in range(EXPERTS):
        expert = where_ref[0] * EXPERTS + ((where_ref[1] + d) & (EXPERTS - 1))
        slots.append(expert_lanes(meta, expert, spread)[0])
    shift = 8.0 * node.astype(F32)
    held = [[None] * EXPERTS for _ in range(chunk.pieces)]
    for g in range(nodes // GROUP):
        lines = [own_lane(slots[d], node, g) + shift for d in range(EXPERTS)]
        picks = []
        for q in range(chunk.pieces):
            for d in range(EXPERTS):
                line = jnp.where(piece == q, lines[d], -9.0)
                picks.append(ones_where(target == line))
        picked = dot(
            jnp.concatenate(picks, axis=0).astype(BF), rows_ref[g * chunk.group : (g + 1) * chunk.group, :]
        )
        height = GROUP * SLOTS
        for q in range(chunk.pieces):
            for d in range(EXPERTS):
                at = (q * EXPERTS + d) * height
                part = picked[at : at + height]
                if g % 2 == 0:
                    held[q][d] = part
                else:
                    both = jnp.concatenate([held[q][d], part], axis=0).astype(BF)
                    out_refs[d][(g - 1) * height : (g + 1) * height, q * width : (q + 1) * width] = both


def select(where, rows, meta, nodes, chunk):
    with_meta = meta is None
    shapes = [jax.ShapeDtypeStruct((nodes * SLOTS, chunk.span), BF)] * EXPERTS
    if with_meta:
        shapes = [jax.ShapeDtypeStruct((nodes, 256), F32)] + shapes
    out = call(
        functools.partial(select_kernel, chunk, with_meta),
        shapes,
        in_specs=[
            pl.BlockSpec(memory_space=pltpu.SMEM),
        ]
        + [pl.BlockSpec(memory_space=pltpu.VMEM)] * (1 if with_meta else 2),
        cost=20,
        name="select_rows",
    )(where, rows, *(() if with_meta else (meta,)))
    return (out[0], out[1:]) if with_meta else (None, out)


def mix_kernel(chunk, where_ref, meta_ref, *refs):
    out_ref, value_refs = refs[-1], refs[:-1]
    nodes = out_ref.shape[0] // chunk.block
    width = chunk.width
    meta = meta_ref[...]
    node, _, spread = lane_tables(chunk)
    target = row_target(chunk)
    tables = []
    for d in range(EXPERTS):
        expert = where_ref[0] * EXPERTS + ((where_ref[1] + d) & (EXPERTS - 1))
        tables.append(expert_lanes(meta, expert, spread))
    shift = 8.0 * node.astype(F32)
    _, out_piece, _ = block_position((chunk.group, width), 0, chunk)
    height = GROUP * SLOTS
    for g in range(nodes // GROUP):
        gated = []
        values = []
        for d in range(EXPERTS):
            line = own_lane(tables[d][0], node, g) + shift
            gate = own_lane(tables[d][1], node, g)
            gated.append(jnp.where(target == line, jnp.broadcast_to(gate, target.shape), 0.0))
            pair = value_refs[d][(g // 2) * 2 * height : (g // 2 + 1) * 2 * height, :].astype(F32)
            values.append(pair[(g % 2) * height : (g % 2 + 1) * height, :])
        share = lax.dot_general(
            jnp.concatenate(gated, axis=0).astype(BF),
            jnp.concatenate(values, axis=0).astype(BF),
            (((0,), (0,)), ((), ())),
            preferred_element_type=F32,
        )
        total = jnp.zeros((chunk.group, width), F32)
        for q in range(chunk.pieces):
            total = jnp.where(out_piece == q, share[:, q * width : (q + 1) * width], total)
        out_ref[g * chunk.group : (g + 1) * chunk.group, :] = total.astype(BF)


def mix(where, meta, values, nodes, chunk):
    return call(
        functools.partial(mix_kernel, chunk),
        jax.ShapeDtypeStruct((nodes * chunk.block, chunk.width), BF),
        in_specs=[pl.BlockSpec(memory_space=pltpu.SMEM)]
        + [pl.BlockSpec(memory_space=pltpu.VMEM)] * (1 + len(values)),
        cost=40,
        name="node_share",
    )(where, meta, *values)


def finish_kernel(chunk, ids_ref, home_ref, *refs):
    out_ref = refs[-1]
    at = 0
    if len(refs) > 1:
        at = chunk.start
        out_ref[:, :at] = refs[0][...]
    tokens, top = ids_ref.shape
    nodes = home_ref.shape[0] // chunk.block
    node = iota((tokens, nodes), 1)
    hit = jnp.zeros((tokens, nodes), F32)
    for k in range(top):
        hit = jnp.maximum(hit, ones_where((ids_ref[:, k : k + 1] >> 2) == node))
    before = ones_where(iota((tokens, tokens), 1) < iota((tokens, tokens), 0)).astype(BF)
    code = jnp.where(hit > 0, dot(before, hit.astype(BF)) + 1.0, 0.0).astype(BF)
    lane_node, piece, row = block_position((1, chunk.group), 1, chunk)
    total = jnp.zeros((chunk.pieces * tokens, chunk.width), F32)
    for g in range(nodes // GROUP):
        spread = ones_where(iota((nodes, chunk.group), 0) == lane_node + g * GROUP).astype(BF)
        lanes = dot(code, spread)
        picks = []
        for q in range(chunk.pieces):
            line = jnp.where(piece == q, row + 1, -9).astype(F32)
            picks.append(ones_where(lanes == line))
        total += dot(
            jnp.concatenate(picks, axis=0).astype(BF), home_ref[g * chunk.group : (g + 1) * chunk.group, :]
        )
    for q in range(chunk.pieces):
        column = at + q * chunk.width
        out_ref[:, column : column + chunk.width] = total[q * tokens : (q + 1) * tokens, :].astype(BF)


def finish(ids, home, chunk, *before):
    columns = chunk.span + (chunk.start if before else 0)
    return call(
        functools.partial(finish_kernel, chunk),
        jax.ShapeDtypeStruct((ids.shape[0], columns), BF),
        cost=6,
        name="sum_over_nodes",
    )(ids, home, *before)


def up_kernel(start, down_start, *refs):
    last = down_start is not None
    count = 2 * EXPERTS
    blocks, (gate_ref, up_ref), refs = refs[:count], refs[count : count + 2], refs[count + 2 :]
    if last:
        sums_in, down_ref, refs = refs[:2], refs[2], refs[3:]
        (hidden_ref, other_out), (x_ref, wg_ref, wu_ref, *sums, wd_ref, other_ref, sems) = refs[:2], refs[2:]
    else:
        outs, (x_ref, wg_ref, wu_ref, sems) = refs[:2], refs[2:]
    rows, span = blocks[0].shape
    band = pl.ds(start, span)
    used = iter(range(64))

    def begin(source, target):
        copy = pltpu.make_async_copy(source, target, sems.at[next(used)])
        copy.start()
        return copy

    weights = [begin(gate_ref.at[0, band, :], wg_ref), begin(up_ref.at[0, band, :], wu_ref)]
    order = [EXPERTS, EXPERTS + 2, 0, 2] if last else [0, 2, EXPERTS, EXPERTS + 2]
    loads = {}
    for i in order:
        at = pl.ds(i * rows, 2 * rows)
        loads[i] = [begin(blocks[k], x_ref.at[pl.ds(k * rows, rows), :]) for k in (i, i + 1)]
        if last:
            loads[i] += [begin(source.at[at, :], target.at[at, :]) for source, target in zip(sums_in, sums)]
            if i == order[1]:
                weights_down = begin(down_ref.at[0, :, pl.ds(down_start, other_ref.shape[1])], wd_ref)
    for copy in weights:
        copy.wait()
    for i in order:
        for copy in loads[i]:
            copy.wait()
        at = pl.ds(i * rows, 2 * rows)
        gate = dot(x_ref[at, :], wg_ref[...])
        up = dot(x_ref[at, :], wu_ref[...])
        if last:
            gate += sums[0][at, :]
            up += sums[1][at, :]
            hidden_ref[at, :] = ((gate / (1.0 + jnp.exp(-gate))) * up).astype(BF)
            if i == order[1]:
                weights_down.wait()
                other_ref[...] = dot(hidden_ref[pl.ds(EXPERTS * rows, EXPERTS * rows), :], wd_ref[...]).astype(BF)
                sent = begin(other_ref, other_out)
        else:
            outs[0][at, :] = gate
            outs[1][at, :] = up
    if last:
        sent.wait()


def up_step(blocks, w_gate, w_up, chunk):
    span = chunk.span
    rows = blocks[0].shape[0] * len(blocks)
    units = w_gate.shape[2]
    any_spec = pl.BlockSpec(memory_space=pl.ANY)
    args = list(blocks) + [w_gate, w_up]
    return call(
        functools.partial(up_kernel, chunk.start, None),
        [jax.ShapeDtypeStruct((rows, units), F32)] * 2,
        in_specs=[any_spec] * len(args),
        scratch_shapes=[
            pltpu.VMEM((rows, span), BF),
            pltpu.VMEM((span, units), BF),
            pltpu.VMEM((span, units), BF),
            pltpu.SemaphoreType.DMA((2 + len(blocks),)),
        ],
        cost=1,
        name="gate_up",
    )(*args)


def hidden_step(blocks, w_gate, w_up, sums, w_down, chunk, down_chunk):
    span, down_span = chunk.span, down_chunk.span
    rows = blocks[0].shape[0] * len(blocks)
    units = w_gate.shape[2]
    any_spec = pl.BlockSpec(memory_space=pl.ANY)
    args = list(blocks) + [w_gate, w_up] + list(sums) + [w_down]
    return call(
        functools.partial(up_kernel, chunk.start, down_chunk.start),
        [jax.ShapeDtypeStruct((rows, units), BF), jax.ShapeDtypeStruct((rows // 2, down_span), BF)],
        in_specs=[any_spec] * len(args),
        out_specs=[pl.BlockSpec(memory_space=pltpu.VMEM), any_spec],
        scratch_shapes=[
            pltpu.VMEM((rows, span), BF),
            pltpu.VMEM((span, units), BF),
            pltpu.VMEM((span, units), BF),
            pltpu.VMEM((rows, units), F32),
            pltpu.VMEM((rows, units), F32),
            pltpu.VMEM((units, down_span), BF),
            pltpu.VMEM((rows // 2, down_span), BF),
            pltpu.SemaphoreType.DMA((4 + 3 * len(blocks),)),
        ],
        cost=10,
        name="hidden_down",
    )(*args)


def down_other_kernel(hidden_ref, w_ref, out_ref):
    out_ref[...] = dot(hidden_ref[...], w_ref[0]).astype(BF)


def down_own_kernel(hidden_ref, w_ref, mate_ref, *out_refs):
    mine = dot(hidden_ref[...], w_ref[0]).astype(BF)
    value = (mine.astype(F32) + mate_ref[...].astype(F32)).astype(BF)
    rows = out_refs[0].shape[0]
    for d, out_ref in enumerate(out_refs):
        out_ref[...] = value[d * rows : (d + 1) * rows, :]


def down_other(hidden, w_down, chunk):
    start, span = chunk.start, chunk.span
    tile = 768 if start == 0 else 512
    rows, units = hidden.shape[0] // 2, hidden.shape[1]
    return call(
        down_other_kernel,
        jax.ShapeDtypeStruct((rows, span), BF),
        grid=(span // tile,),
        in_specs=[
            pl.BlockSpec((rows, units), lambda i: (1, 0)),
            pl.BlockSpec((1, units, tile), lambda i: (0, 0, start // tile + i)),
        ],
        out_specs=pl.BlockSpec((rows, tile), lambda i: (0, i)),
        cost=4,
        name="down_other",
    )(hidden, w_down)


def down_own(hidden, w_down, mate, chunk):
    start, span = chunk.start, chunk.span
    tile = 768 if start == 0 else 512
    rows, units = hidden.shape[0] // 2, hidden.shape[1]
    part = rows // EXPERTS
    return call(
        down_own_kernel,
        [jax.ShapeDtypeStruct((part, span), BF)] * EXPERTS,
        grid=(span // tile,),
        in_specs=[
            pl.BlockSpec((rows, units), lambda i: (0, 0)),
            pl.BlockSpec((1, units, tile), lambda i: (0, 0, start // tile + i)),
            pl.BlockSpec((rows, tile), lambda i: (0, i)),
        ],
        out_specs=[pl.BlockSpec((part, tile), lambda i: (0, i))] * EXPERTS,
        cost=10 if chunk.start == 0 else 4,
        name="down_own",
    )(hidden, w_down, mate)


def over_nodes(rows, nodes):
    cut = rows.reshape(nodes, rows.shape[0] // nodes, rows.shape[1])
    return lax.all_to_all(cut, "node", split_axis=0, concat_axis=0, tiled=True).reshape(rows.shape)


def along_y(block, distance):
    pairs = [(y * 2 + c, ((y + distance) % EXPERTS) * 2 + c) for y in range(EXPERTS) for c in range(2)]
    return lax.ppermute(block, "local", pairs)


def to_mate(block):
    return lax.ppermute(block, "local", [(i, i ^ 1) for i in range(2 * EXPERTS)])


def per_device(tokens, expert_ids, gate_weights, w_gate, w_up, w_down):
    nodes = lax.axis_size("node")
    where = jnp.stack([lax.axis_index("node"), lax.axis_index("local") // 2]).astype(jnp.int32)
    ids_t = expert_ids.T
    gates_t = gate_weights.T
    packed = [pack(ids_t, gates_t, tokens, nodes, chunk, chunk is OUT[0]) for chunk in OUT]
    packed[1], where = lax.optimization_barrier((packed[1], where))
    arrived = [over_nodes(rows, nodes) for rows in packed]
    meta, blocks = select(where, arrived[0], None, nodes, OUT[0])
    own = [blocks[0]] + [along_y(blocks[d], d) for d in range(1, EXPERTS)]
    near = to_mate(blocks[0])
    _, blocks = select(where, arrived[1], meta, nodes, OUT[1])
    own, near, blocks = lax.optimization_barrier((own, near, blocks))
    later = [along_y(blocks[d], d) for d in range(1, EXPERTS)]
    later_near = to_mate(blocks[0])
    sums = up_step(own + [near] + [to_mate(block) for block in own[1:]], w_gate, w_up, OUT[0])
    later, sums = lax.optimization_barrier((later, sums))
    own = [blocks[0]] + later
    hidden, other = hidden_step(
        own + [later_near] + [to_mate(block) for block in later], w_gate, w_up, sums, w_down, OUT[1], HOME[0]
    )
    mate = to_mate(other)
    later_mate = to_mate(down_other(hidden, w_down, HOME[1]))
    values = down_own(hidden, w_down, mate, HOME[0])
    back = [values[0]] + [along_y(values[d], -d) for d in range(1, EXPERTS)]
    values = down_own(hidden, w_down, later_mate, HOME[1])
    later_back = [values[0]] + [along_y(values[d], -d) for d in range(1, EXPERTS)]
    home = over_nodes(mix(where, meta, back, nodes, HOME[0]), nodes)
    later_home = over_nodes(mix(where, meta, later_back, nodes, HOME[1]), nodes)
    return finish(expert_ids, later_home, HOME[1], finish(expert_ids, home, HOME[0]))


def solution(mesh):
    rows = P(("node", "local"), None)
    cube = P(("node", "local"), None, None)
    return jax.shard_map(
        per_device,
        mesh=mesh,
        in_specs=(rows, rows, rows, cube, cube, cube),
        out_specs=rows,
        check_vma=False,
    )
```

```python
import functools
from typing import NamedTuple

import jax
import jax.numpy as jnp
from jax import lax
from jax.experimental import pallas as pl
from jax.experimental.pallas import tpu as pltpu
from jax.sharding import PartitionSpec as P

SLOTS = 5
EXPERTS = 4
NODE_ROWS = EXPERTS * SLOTS // 2
GROUP = 8


class Chunk(NamedTuple):
    start: int
    width: int
    pieces: int
    block: int

    @property
    def span(self):
        return self.width * self.pieces

    @property
    def group(self):
        return self.block * GROUP


OUT = (Chunk(0, 512, 3, 32), Chunk(1536, 512, 4, 40))
HOME = (Chunk(0, 384, 4, 40), Chunk(1536, 512, 4, 40))
BF = jnp.bfloat16
F32 = jnp.float32
VMEM = 63 << 20


def dot(a, b):
    return jnp.dot(a, b, preferred_element_type=F32)


def iota(shape, dim):
    return lax.broadcasted_iota(jnp.int32, shape, dim)


def steps(value, step, count):
    total = jnp.zeros_like(value)
    for i in range(1, count):
        total = total + jnp.where(value >= step * i, 1, 0)
    return total


def ones_where(mask):
    return jnp.where(mask, 1.0, 0.0).astype(F32)


def block_position(shape, dim, chunk):
    index = iota(shape, dim)
    node = steps(index, chunk.block, GROUP)
    inner = index - chunk.block * node
    piece = steps(inner, NODE_ROWS, chunk.pieces + 1)
    return node, piece, inner - NODE_ROWS * piece


def call(kernel, out_shape, cost, **kwargs):
    return pl.pallas_call(
        kernel,
        out_shape=out_shape,
        cost_estimate=pl.CostEstimate(flops=cost * 10**9, bytes_accessed=10**6, transcendentals=0),
        compiler_params=pltpu.CompilerParams(vmem_limit_bytes=VMEM),
        **kwargs,
    )


def node_code(ids, nodes):
    node = iota((nodes, ids.shape[1]), 0)
    hit = jnp.zeros(node.shape, F32)
    for k in range(ids.shape[0]):
        hit = jnp.maximum(hit, ones_where((ids[k : k + 1, :] >> 2) == node))
    tokens = ids.shape[1]
    before = ones_where(iota((tokens, tokens), 0) < iota((tokens, tokens), 1)).astype(BF)
    return jnp.where(hit > 0, dot(hit.astype(BF), before), -1.0)


def row_meta(ids, gates, code):
    top, tokens = ids.shape
    expert = iota((128, tokens), 0)
    hits = [ones_where(ids[k : k + 1, :] == expert) for k in range(top)]
    before = ones_where(iota((tokens, tokens), 0) < iota((tokens, tokens), 1)).astype(BF)
    rank = dot(functools.reduce(jnp.maximum, hits).astype(BF), before)
    items = [(ids[k : k + 1, :] + 1).astype(F32) for k in range(top)]
    items += [jnp.sum(hits[k] * rank, axis=0, keepdims=True) for k in range(top)]
    items += [gates[k : k + 1, :] for k in range(top)]
    table = jnp.concatenate(
        [jnp.broadcast_to(item, (16, tokens)) for item in items]
        + [jnp.zeros((256 - 16 * len(items), tokens), F32)],
        axis=0,
    )
    place = iota(table.shape, 0) & 15
    meta = jnp.zeros((code.shape[0], 256), F32)
    for r in range(NODE_ROWS):
        meta += lax.dot_general(
            ones_where(code == float(r)).astype(BF),
            jnp.where(place == r, table, 0.0).astype(BF),
            (((1,), (1,)), ((), ())),
            preferred_element_type=F32,
        )
    return meta.astype(BF)


def pack_kernel(chunk, with_meta, ids_ref, gates_ref, tok_ref, out_ref):
    ids = ids_ref[...]
    nodes = out_ref.shape[0] // chunk.block
    tokens = ids.shape[1]
    code = node_code(ids, nodes)
    inner = iota((chunk.block, tokens), 0)
    piece = steps(inner, NODE_ROWS, chunk.pieces + 1)
    row = (inner - NODE_ROWS * piece).astype(F32)
    wanted = [jnp.where(piece == q, row, -9.0) for q in range(chunk.pieces)]
    first = [chunk.start + q * chunk.width for q in range(chunk.pieces)]
    stacked = jnp.concatenate([tok_ref[:, at : at + chunk.width] for at in first], axis=0)
    if with_meta:
        meta = row_meta(ids, gates_ref[...].astype(F32), code)
        meta = jnp.concatenate([meta, jnp.zeros((nodes, chunk.width - 256), BF)], axis=1)
        node_of = steps(iota((chunk.group, nodes), 0), chunk.block, GROUP)
        inner_of = iota((chunk.group, nodes), 0) - chunk.block * node_of
    for g in range(nodes // GROUP):
        picks = []
        for q in range(chunk.pieces):
            picks.append(
                jnp.concatenate(
                    [ones_where(code[n : n + 1, :] == wanted[q]) for n in range(g * GROUP, (g + 1) * GROUP)],
                    axis=0,
                ).astype(BF)
            )
        rows = dot(jnp.concatenate(picks, axis=1), stacked)
        if with_meta:
            spot = (node_of + g * GROUP == iota((chunk.group, nodes), 1)) & (inner_of == chunk.pieces * NODE_ROWS)
            rows += dot(ones_where(spot).astype(BF), meta)
        out_ref[g * chunk.group : (g + 1) * chunk.group, :] = rows.astype(BF)


def pack(ids_t, gates_t, tokens, nodes, chunk, with_meta):
    return call(
        functools.partial(pack_kernel, chunk, with_meta),
        jax.ShapeDtypeStruct((nodes * chunk.block, chunk.width), BF),
        cost=5,
        name="pack_rows",
    )(ids_t, gates_t, tokens)


def expert_lanes(meta, expert, spread):
    ids = meta[:, :128]
    hit = ones_where(ids == (expert + 1).astype(F32))
    slot = dot((hit * (pltpu.roll(ids, 64, 1) + 1.0)).astype(BF), spread)
    gate = dot((hit * meta[:, 128:256]).astype(BF), spread)
    return slot, gate


def own_lane(values, node, g):
    part = values[g * GROUP : (g + 1) * GROUP, :]
    return jnp.sum(jnp.where(iota(part.shape, 0) == node, part, 0.0), axis=0, keepdims=True)


def lane_tables(chunk):
    node, piece, row = block_position((1, chunk.group), 1, chunk)
    lane = iota((128, chunk.group), 0)
    spread = ones_where(((lane & 15) == row) & (lane < 64)).astype(BF)
    return node, piece, spread


def row_target(chunk):
    row = iota((GROUP * SLOTS, chunk.group), 0)
    node = steps(row, SLOTS, GROUP)
    return (row + (8 - SLOTS) * node + 1).astype(F32)


def select_kernel(chunk, with_meta, where_ref, rows_ref, *out_refs):
    nodes = rows_ref.shape[0] // chunk.block
    width = chunk.width
    if with_meta:
        meta_ref, out_refs = out_refs[0], out_refs[1:]
        shape = (nodes, rows_ref.shape[0])
        spot = iota(shape, 1) == iota(shape, 0) * chunk.block + chunk.pieces * NODE_ROWS
        meta = dot(ones_where(spot).astype(BF), rows_ref[:, :256])
        meta_ref[...] = meta
    else:
        meta, out_refs = out_refs[0][...], out_refs[1:]
    node, piece, spread = lane_tables(chunk)
    target = row_target(chunk)
    slots = []
    for d in range(EXPERTS):
        expert = where_ref[0] * EXPERTS + ((where_ref[1] + d) & (EXPERTS - 1))
        slots.append(expert_lanes(meta, expert, spread)[0])
    shift = 8.0 * node.astype(F32)
    held = [[None] * EXPERTS for _ in range(chunk.pieces)]
    for g in range(nodes // GROUP):
        lines = [own_lane(slots[d], node, g) + shift for d in range(EXPERTS)]
        picks = []
        for q in range(chunk.pieces):
            for d in range(EXPERTS):
                line = jnp.where(piece == q, lines[d], -9.0)
                picks.append(ones_where(target == line))
        picked = dot(
            jnp.concatenate(picks, axis=0).astype(BF), rows_ref[g * chunk.group : (g + 1) * chunk.group, :]
        )
        height = GROUP * SLOTS
        for q in range(chunk.pieces):
            for d in range(EXPERTS):
                at = (q * EXPERTS + d) * height
                part = picked[at : at + height]
                if g % 2 == 0:
                    held[q][d] = part
                else:
                    both = jnp.concatenate([held[q][d], part], axis=0).astype(BF)
                    out_refs[d][(g - 1) * height : (g + 1) * height, q * width : (q + 1) * width] = both


def select(where, rows, meta, nodes, chunk):
    with_meta = meta is None
    shapes = [jax.ShapeDtypeStruct((nodes * SLOTS, chunk.span), BF)] * EXPERTS
    if with_meta:
        shapes = [jax.ShapeDtypeStruct((nodes, 256), F32)] + shapes
    out = call(
        functools.partial(select_kernel, chunk, with_meta),
        shapes,
        in_specs=[
            pl.BlockSpec(memory_space=pltpu.SMEM),
        ]
        + [pl.BlockSpec(memory_space=pltpu.VMEM)] * (1 if with_meta else 2),
        cost=20,
        name="select_rows",
    )(where, rows, *(() if with_meta else (meta,)))
    return (out[0], out[1:]) if with_meta else (None, out)


def mix_kernel(chunk, where_ref, meta_ref, *refs):
    out_ref, value_refs = refs[-1], refs[:-1]
    nodes = out_ref.shape[0] // chunk.block
    width = chunk.width
    meta = meta_ref[...]
    node, _, spread = lane_tables(chunk)
    target = row_target(chunk)
    tables = []
    for d in range(EXPERTS):
        expert = where_ref[0] * EXPERTS + ((where_ref[1] + d) & (EXPERTS - 1))
        tables.append(expert_lanes(meta, expert, spread))
    shift = 8.0 * node.astype(F32)
    _, out_piece, _ = block_position((chunk.group, width), 0, chunk)
    height = GROUP * SLOTS
    for g in range(nodes // GROUP):
        gated = []
        values = []
        for d in range(EXPERTS):
            line = own_lane(tables[d][0], node, g) + shift
            gate = own_lane(tables[d][1], node, g)
            gated.append(jnp.where(target == line, jnp.broadcast_to(gate, target.shape), 0.0))
            pair = value_refs[d][(g // 2) * 2 * height : (g // 2 + 1) * 2 * height, :].astype(F32)
            values.append(pair[(g % 2) * height : (g % 2 + 1) * height, :])
        share = lax.dot_general(
            jnp.concatenate(gated, axis=0).astype(BF),
            jnp.concatenate(values, axis=0).astype(BF),
            (((0,), (0,)), ((), ())),
            preferred_element_type=F32,
        )
        total = jnp.zeros((chunk.group, width), F32)
        for q in range(chunk.pieces):
            total = jnp.where(out_piece == q, share[:, q * width : (q + 1) * width], total)
        out_ref[g * chunk.group : (g + 1) * chunk.group, :] = total.astype(BF)


def mix(where, meta, values, nodes, chunk):
    return call(
        functools.partial(mix_kernel, chunk),
        jax.ShapeDtypeStruct((nodes * chunk.block, chunk.width), BF),
        in_specs=[pl.BlockSpec(memory_space=pltpu.SMEM)]
        + [pl.BlockSpec(memory_space=pltpu.VMEM)] * (1 + len(values)),
        cost=40,
        name="node_share",
    )(where, meta, *values)


def finish_kernel(chunk, ids_ref, home_ref, *refs):
    out_ref = refs[-1]
    at = 0
    if len(refs) > 1:
        at = chunk.start
        out_ref[:, :at] = refs[0][...]
    tokens, top = ids_ref.shape
    nodes = home_ref.shape[0] // chunk.block
    node = iota((tokens, nodes), 1)
    hit = jnp.zeros((tokens, nodes), F32)
    for k in range(top):
        hit = jnp.maximum(hit, ones_where((ids_ref[:, k : k + 1] >> 2) == node))
    before = ones_where(iota((tokens, tokens), 1) < iota((tokens, tokens), 0)).astype(BF)
    code = jnp.where(hit > 0, dot(before, hit.astype(BF)) + 1.0, 0.0).astype(BF)
    lane_node, piece, row = block_position((1, chunk.group), 1, chunk)
    total = jnp.zeros((chunk.pieces * tokens, chunk.width), F32)
    for g in range(nodes // GROUP):
        spread = ones_where(iota((nodes, chunk.group), 0) == lane_node + g * GROUP).astype(BF)
        lanes = dot(code, spread)
        picks = []
        for q in range(chunk.pieces):
            line = jnp.where(piece == q, row + 1, -9).astype(F32)
            picks.append(ones_where(lanes == line))
        total += dot(
            jnp.concatenate(picks, axis=0).astype(BF), home_ref[g * chunk.group : (g + 1) * chunk.group, :]
        )
    for q in range(chunk.pieces):
        column = at + q * chunk.width
        out_ref[:, column : column + chunk.width] = total[q * tokens : (q + 1) * tokens, :].astype(BF)


def finish(ids, home, chunk, *before):
    columns = chunk.span + (chunk.start if before else 0)
    return call(
        functools.partial(finish_kernel, chunk),
        jax.ShapeDtypeStruct((ids.shape[0], columns), BF),
        cost=6,
        name="sum_over_nodes",
    )(ids, home, *before)


def up_kernel(start, down_start, *refs):
    last = down_start is not None
    count = 2 * EXPERTS
    blocks, (gate_ref, up_ref), refs = refs[:count], refs[count : count + 2], refs[count + 2 :]
    if last:
        sums_in, down_ref, refs = refs[:2], refs[2], refs[3:]
        (hidden_ref, other_out), (x_ref, wg_ref, wu_ref, *sums, wd_ref, other_ref, sems) = refs[:2], refs[2:]
    else:
        outs, (x_ref, wg_ref, wu_ref, sems) = refs[:2], refs[2:]
    rows, span = blocks[0].shape
    band = pl.ds(start, span)
    used = iter(range(64))

    def begin(source, target):
        copy = pltpu.make_async_copy(source, target, sems.at[next(used)])
        copy.start()
        return copy

    weights = [begin(gate_ref.at[0, band, :], wg_ref), begin(up_ref.at[0, band, :], wu_ref)]
    order = [EXPERTS, EXPERTS + 2, 0, 2] if last else [0, 2, EXPERTS, EXPERTS + 2]
    loads = {}
    for i in order:
        at = pl.ds(i * rows, 2 * rows)
        loads[i] = [begin(blocks[k], x_ref.at[pl.ds(k * rows, rows), :]) for k in (i, i + 1)]
        if last:
            loads[i] += [begin(source.at[at, :], target.at[at, :]) for source, target in zip(sums_in, sums)]
            if i == order[1]:
                weights_down = begin(down_ref.at[0, :, pl.ds(down_start, other_ref.shape[1])], wd_ref)
    for copy in weights:
        copy.wait()
    for i in order:
        for copy in loads[i]:
            copy.wait()
        at = pl.ds(i * rows, 2 * rows)
        gate = dot(x_ref[at, :], wg_ref[...])
        up = dot(x_ref[at, :], wu_ref[...])
        if last:
            gate += sums[0][at, :]
            up += sums[1][at, :]
            hidden_ref[at, :] = ((gate / (1.0 + jnp.exp(-gate))) * up).astype(BF)
            if i == order[1]:
                weights_down.wait()
                other_ref[...] = dot(hidden_ref[pl.ds(EXPERTS * rows, EXPERTS * rows), :], wd_ref[...]).astype(BF)
                sent = begin(other_ref, other_out)
        else:
            outs[0][at, :] = gate
            outs[1][at, :] = up
    if last:
        sent.wait()


def up_step(blocks, w_gate, w_up, chunk):
    span = chunk.span
    rows = blocks[0].shape[0] * len(blocks)
    units = w_gate.shape[2]
    any_spec = pl.BlockSpec(memory_space=pl.ANY)
    args = list(blocks) + [w_gate, w_up]
    return call(
        functools.partial(up_kernel, chunk.start, None),
        [jax.ShapeDtypeStruct((rows, units), F32)] * 2,
        in_specs=[any_spec] * len(args),
        scratch_shapes=[
            pltpu.VMEM((rows, span), BF),
            pltpu.VMEM((span, units), BF),
            pltpu.VMEM((span, units), BF),
            pltpu.SemaphoreType.DMA((2 + len(blocks),)),
        ],
        cost=1,
        name="gate_up",
    )(*args)


def hidden_step(blocks, w_gate, w_up, sums, w_down, chunk, down_chunk):
    span, down_span = chunk.span, down_chunk.span
    rows = blocks[0].shape[0] * len(blocks)
    units = w_gate.shape[2]
    any_spec = pl.BlockSpec(memory_space=pl.ANY)
    args = list(blocks) + [w_gate, w_up] + list(sums) + [w_down]
    return call(
        functools.partial(up_kernel, chunk.start, down_chunk.start),
        [jax.ShapeDtypeStruct((rows, units), BF), jax.ShapeDtypeStruct((rows // 2, down_span), BF)],
        in_specs=[any_spec] * len(args),
        out_specs=[pl.BlockSpec(memory_space=pltpu.VMEM), any_spec],
        scratch_shapes=[
            pltpu.VMEM((rows, span), BF),
            pltpu.VMEM((span, units), BF),
            pltpu.VMEM((span, units), BF),
            pltpu.VMEM((rows, units), F32),
            pltpu.VMEM((rows, units), F32),
            pltpu.VMEM((units, down_span), BF),
            pltpu.VMEM((rows // 2, down_span), BF),
            pltpu.SemaphoreType.DMA((4 + 3 * len(blocks),)),
        ],
        cost=10,
        name="hidden_down",
    )(*args)


def down_other_kernel(hidden_ref, w_ref, out_ref):
    out_ref[...] = dot(hidden_ref[...], w_ref[0]).astype(BF)


def down_own_kernel(hidden_ref, w_ref, mate_ref, *out_refs):
    mine = dot(hidden_ref[...], w_ref[0]).astype(BF)
    value = (mine.astype(F32) + mate_ref[...].astype(F32)).astype(BF)
    rows = out_refs[0].shape[0]
    for d, out_ref in enumerate(out_refs):
        out_ref[...] = value[d * rows : (d + 1) * rows, :]


def down_other(hidden, w_down, chunk):
    start, span = chunk.start, chunk.span
    tile = 768 if start == 0 else 512
    rows, units = hidden.shape[0] // 2, hidden.shape[1]
    return call(
        down_other_kernel,
        jax.ShapeDtypeStruct((rows, span), BF),
        grid=(span // tile,),
        in_specs=[
            pl.BlockSpec((rows, units), lambda i: (1, 0)),
            pl.BlockSpec((1, units, tile), lambda i: (0, 0, start // tile + i)),
        ],
        out_specs=pl.BlockSpec((rows, tile), lambda i: (0, i)),
        cost=4,
        name="down_other",
    )(hidden, w_down)


def down_own(hidden, w_down, mate, chunk):
    start, span = chunk.start, chunk.span
    tile = 768 if start == 0 else 512
    rows, units = hidden.shape[0] // 2, hidden.shape[1]
    part = rows // EXPERTS
    return call(
        down_own_kernel,
        [jax.ShapeDtypeStruct((part, span), BF)] * EXPERTS,
        grid=(span // tile,),
        in_specs=[
            pl.BlockSpec((rows, units), lambda i: (0, 0)),
            pl.BlockSpec((1, units, tile), lambda i: (0, 0, start // tile + i)),
            pl.BlockSpec((rows, tile), lambda i: (0, i)),
        ],
        out_specs=[pl.BlockSpec((part, tile), lambda i: (0, i))] * EXPERTS,
        cost=10 if chunk.start == 0 else 4,
        name="down_own",
    )(hidden, w_down, mate)


def over_nodes(rows, nodes):
    cut = rows.reshape(nodes, rows.shape[0] // nodes, rows.shape[1])
    return lax.all_to_all(cut, "node", split_axis=0, concat_axis=0, tiled=True).reshape(rows.shape)


def along_y(block, distance):
    pairs = [(y * 2 + c, ((y + distance) % EXPERTS) * 2 + c) for y in range(EXPERTS) for c in range(2)]
    return lax.ppermute(block, "local", pairs)


def to_mate(block):
    return lax.ppermute(block, "local", [(i, i ^ 1) for i in range(2 * EXPERTS)])


def per_device(tokens, expert_ids, gate_weights, w_gate, w_up, w_down):
    nodes = lax.axis_size("node")
    where = jnp.stack([lax.axis_index("node"), lax.axis_index("local") // 2]).astype(jnp.int32)
    ids_t = expert_ids.T
    gates_t = gate_weights.T
    packed = [pack(ids_t, gates_t, tokens, nodes, chunk, chunk is OUT[0]) for chunk in OUT]
    packed[1], where = lax.optimization_barrier((packed[1], where))
    arrived = [over_nodes(rows, nodes) for rows in packed]
    meta, blocks = select(where, arrived[0], None, nodes, OUT[0])
    own = [blocks[0]] + [along_y(blocks[d], d) for d in range(1, EXPERTS)]
    near = to_mate(blocks[0])
    _, blocks = select(where, arrived[1], meta, nodes, OUT[1])
    own, near, blocks = lax.optimization_barrier((own, near, blocks))
    later = [along_y(blocks[d], d) for d in range(1, EXPERTS)]
    later_near = to_mate(blocks[0])
    sums = up_step(own + [near] + [to_mate(block) for block in own[1:]], w_gate, w_up, OUT[0])
    later, sums = lax.optimization_barrier((later, sums))
    own = [blocks[0]] + later
    hidden, other = hidden_step(
        own + [later_near] + [to_mate(block) for block in later], w_gate, w_up, sums, w_down, OUT[1], HOME[0]
    )
    mate = to_mate(other)
    later_mate = to_mate(down_other(hidden, w_down, HOME[1]))
    values = down_own(hidden, w_down, mate, HOME[0])
    back = [values[0]] + [along_y(values[d], -d) for d in range(1, EXPERTS)]
    values = down_own(hidden, w_down, later_mate, HOME[1])
    back[1], values = lax.optimization_barrier((back[1], values))
    later_back = [values[0]] + [along_y(values[d], -d) for d in range(1, EXPERTS)]
    home = over_nodes(mix(where, meta, back, nodes, HOME[0]), nodes)
    later_home = over_nodes(mix(where, meta, later_back, nodes, HOME[1]), nodes)
    return finish(expert_ids, later_home, HOME[1], finish(expert_ids, home, HOME[0]))


def solution(mesh):
    rows = P(("node", "local"), None)
    cube = P(("node", "local"), None, None)
    return jax.shard_map(
        per_device,
        mesh=mesh,
        in_specs=(rows, rows, rows, cube, cube, cube),
        out_specs=rows,
        check_vma=False,
    )
```
